128 devices in a mesh: dp: 8 (over z, core), fsdp: 16 (over x, y).
Axes of the slice: x: 4, y: 4, z: 4, core: 2. Of those that a mesh axis runs over, the one named last changes fastest.
Arguments:
- grads: bfloat16 [8, 224, 512, 512], P('dp', 'fsdp'), may hold values from -1 to 1
- owner: int32 [224], replicated, may hold values from 0 to 15, as said below
- roster: int32 [224], replicated, may hold values from 0 to 1, as said below
- left_stats: float32 [8, 16, 2, 512, 512], P('dp', 'fsdp'), may hold values from -1 to 20, as said below
- right_stats: float32 [8, 16, 2, 512, 512], P('dp', 'fsdp'), may hold values from -1 to 20, as said below
- left_root: bfloat16 [8, 16, 2, 512, 512], P('dp', 'fsdp'), may hold values from -1 to 6, as said below
- right_root: bfloat16 [8, 16, 2, 512, 512], P('dp', 'fsdp'), may hold values from -1 to 6, as said below
Outputs:
- updates: bfloat16 [224, 512, 512], P('fsdp', 'dp')
- new_left_stats: float32 [8, 16, 2, 512, 512], P('dp', 'fsdp')
- new_right_stats: float32 [8, 16, 2, 512, 512], P('dp', 'fsdp')
- new_left_root: bfloat16 [8, 16, 2, 512, 512], P('dp', 'fsdp')
- new_right_root: bfloat16 [8, 16, 2, 512, 512], P('dp', 'fsdp')
The draws below stay inside these ranges and needn't reach their ends.
Inputs may be any that keep to these rules, and one draw needn't show every extreme that they name: `owner`: the 14 entries of one home (entries h * 14 to h * 14 + 13) name 14 different owners. `roster`: exactly 112 entries are 1. `left_stats`: every matrix is symmetric positive definite. `right_stats`: every matrix is symmetric positive definite. `left_root`: every matrix is symmetric positive definite. `right_root`: every matrix is symmetric positive definite.
All inputs are finite; a program needn't handle non-finite values. Where the reference program divides by a largest or mean magnitude, that divisor is 1e-20 or more.
Results may differ from the reference program's by a relative error of at most 0.02.
Values may be sent and summed in bfloat16 or wider, within the bound.
A program may use at most 128 MiB of HBM per device.

```python
import math
import jax
import jax.numpy as jnp
from jax import lax

BS = 512
NEWTON = 4
HOMEB = 14
NB = 224
SPAIR = 2
N_DP = 8
N_FSDP = 16


def spd_matrices(key, leading, size, lowest, highest, coupling):
    key_scale, key_point, key_noise = jax.random.split(key, 3)
    scales = jnp.exp(jax.random.uniform(key_scale, leading + (size,), jnp.float32, math.log(lowest), math.log(highest)))
    points = jax.random.uniform(key_point, leading + (size,), jnp.float32, 0.0, 1.0)
    radius = 4.0 / size
    kernel = jnp.exp(-jnp.abs(points[..., :, None] - points[..., None, :]) / radius)
    noise = jax.random.uniform(key_noise, leading + (size, size), jnp.float32, -1.0, 1.0) * (0.5 / (size - 1))
    symmetric = 0.5 * (noise + jnp.swapaxes(noise, -1, -2))
    identity = jnp.eye(size, dtype=jnp.float32)
    centre = identity + coupling * kernel + symmetric * (1.0 - identity)
    return scales[..., :, None] * centre * scales[..., None, :]


def draw_grads(key, part):
    key = jax.random.fold_in(key, 17)
    key_rows, key_cols, key_noise = jax.random.split(key, 3)
    rows = jnp.exp(jax.random.uniform(key_rows, (NB, BS), jnp.float32, math.log(0.3), math.log(3.0)))
    cols = jnp.exp(jax.random.uniform(key_cols, (NB, BS), jnp.float32, math.log(0.3), math.log(3.0)))
    noise = jax.random.truncated_normal(key_noise, -4.0, 4.0, (N_DP, NB, BS, BS), jnp.float32)
    values = 0.0156 * noise * rows[None, :, :, None] * cols[None, :, None, :]
    return values.astype(jnp.bfloat16)


def draw_owner(key, part):
    key = jax.random.fold_in(key, 19)
    home_keys = jax.random.split(key, N_FSDP)
    orders = jax.vmap(lambda single: jax.random.permutation(single, N_FSDP))(home_keys)
    return orders[:, :HOMEB].reshape(NB).astype(jnp.int32)


def draw_roster(key, part):
    key = jax.random.fold_in(key, 23)
    order = jax.random.permutation(key, NB)
    return (order < NB // 2).astype(jnp.int32)


def draw_left_stats(key, part):
    key = jax.random.fold_in(key, 29)
    return spd_matrices(key, (N_DP, N_FSDP, SPAIR), BS, 0.7, 2.24, 1.0)


def draw_right_stats(key, part):
    key = jax.random.fold_in(key, 31)
    return spd_matrices(key, (N_DP, N_FSDP, SPAIR), BS, 0.7, 2.24, 1.0)


def draw_left_root(key, part):
    key = jax.random.fold_in(key, 37)
    return spd_matrices(key, (N_DP, N_FSDP, SPAIR), BS, 0.6, 1.4, 0.6).astype(jnp.bfloat16)


def draw_right_root(key, part):
    key = jax.random.fold_in(key, 41)
    return spd_matrices(key, (N_DP, N_FSDP, SPAIR), BS, 0.6, 1.4, 0.6).astype(jnp.bfloat16)


def setup_inputs(seed: int = 0) -> dict:
    splits = jax.random.split(jax.random.key(seed), 8)
    return {
        "grads": draw_grads(jax.random.fold_in(splits[7], 71), 0),
        "owner": draw_owner(jax.random.fold_in(splits[7], 71), 0),
        "roster": draw_roster(jax.random.fold_in(splits[7], 71), 0),
        "left_stats": draw_left_stats(jax.random.fold_in(splits[7], 71), 0),
        "right_stats": draw_right_stats(jax.random.fold_in(splits[7], 71), 0),
        "left_root": draw_left_root(jax.random.fold_in(splits[7], 71), 0),
        "right_root": draw_right_root(jax.random.fold_in(splits[7], 71), 0),
    }


decay_rate = 0.9
learn_rate = 10.0

def inverse_root(stats):
    bound = jnp.max(lax.optimization_barrier(jnp.sum(jnp.abs(stats), axis=1)))
    identity = jnp.eye(stats.shape[0], dtype=jnp.float32)
    scaled = stats / bound
    current = identity * bound ** (-0.25)
    for sweep in range(NEWTON):
        factor = ((5.0 * identity - scaled) * 0.25).astype(jnp.bfloat16)
        current = jnp.dot(current.astype(jnp.bfloat16), factor, preferred_element_type=jnp.float32)
        if sweep + 1 < NEWTON:
            square = jnp.dot(factor, factor, preferred_element_type=jnp.float32).astype(jnp.bfloat16)
            fourth = jnp.dot(square, square, preferred_element_type=jnp.float32).astype(jnp.bfloat16)
            scaled = jnp.dot(fourth, scaled.astype(jnp.bfloat16), preferred_element_type=jnp.float32)
    return current.astype(jnp.bfloat16)

def process_slot(operands):
    grad, left, right, keep_left, keep_right, flag = operands
    grad_bf = grad.astype(jnp.bfloat16)
    new_left = decay_rate * left + (1.0 - decay_rate) * jnp.dot(grad_bf, grad_bf.T, preferred_element_type=jnp.float32)
    new_right = decay_rate * right + (1.0 - decay_rate) * jnp.dot(grad_bf.T, grad_bf, preferred_element_type=jnp.float32)
    root_left, root_right = lax.cond(flag > 0.5, lambda: (inverse_root(left), inverse_root(right)), lambda: (keep_left, keep_right))
    half = jnp.dot(root_left, grad_bf, preferred_element_type=jnp.float32).astype(jnp.bfloat16)
    direction = jnp.dot(half, root_right, preferred_element_type=jnp.float32)
    grad_scale = jnp.sqrt(jnp.mean(grad * grad))
    dir_scale = jnp.sqrt(jnp.mean(direction * direction) + 1e-06)
    update = (-learn_rate * direction * (grad_scale / dir_scale)).astype(jnp.bfloat16)
    return (new_left, new_right, root_left, root_right, update)

def to_source_major(stack):
    return jnp.transpose(stack, (0, 2, 1, 3, 4)).reshape(N_FSDP * N_FSDP, BS, BS)

def to_slot_layout(stack):
    return jnp.transpose(stack.reshape(N_DP, SPAIR, N_FSDP, BS, BS), (0, 2, 1, 3, 4))

def reference(grads, owner, roster, left_stats, right_stats, left_root, right_root):
    summed = lax.optimization_barrier(jnp.sum(grads, axis=0, dtype=jnp.float32))
    homes = summed.reshape(N_FSDP, HOMEB, BS, BS)
    table = owner.reshape(N_FSDP, HOMEB)
    owner_ids = jnp.arange(N_FSDP, dtype=jnp.int32)
    picks = (table[:, :, None] == owner_ids[None, None, :]).astype(jnp.float32)
    slot_grad = jnp.einsum('sko,skij->soij', picks, homes).reshape(N_FSDP * N_FSDP, BS, BS)
    plan = roster.reshape(N_FSDP, HOMEB).astype(jnp.float32)
    slot_flag = jnp.einsum('sko,sk->so', picks, plan).reshape(N_FSDP * N_FSDP)
    results = lax.map(process_slot, (slot_grad, to_source_major(left_stats), to_source_major(right_stats), to_source_major(left_root), to_source_major(right_root), slot_flag))
    new_left, new_right, root_left, root_right, slot_update = results
    slot_update = slot_update.astype(jnp.float32).reshape(N_FSDP, N_FSDP, BS, BS)
    updates = jnp.einsum('sko,soij->skij', picks, slot_update).astype(jnp.bfloat16).reshape(NB, BS, BS)
    return (updates, to_slot_layout(new_left), to_slot_layout(new_right), to_slot_layout(root_left), to_slot_layout(root_right))
```

```python
import jax
import jax.numpy as jnp
from jax import lax
from jax.experimental import pallas as pl
from jax.experimental.pallas import tpu as pltpu
from jax.sharding import PartitionSpec as P

BS = 512
HOMEB = 14
HALF = HOMEB // 2
NZ = 4
N_DP = 8
N_FSDP = 16
ROWS = BS // N_DP
R = 4
RR = ROWS // R
ROOT_STEPS = 6
decay_rate = 0.9
learn_rate = 10.0
BF = jnp.bfloat16
F32 = jnp.float32
MESH = pl.DeviceIdType.MESH


def dot(a, b, ca=1, cb=0):
    return lax.dot_general(a, b, (((ca,), (cb,)), ((), ())), preferred_element_type=F32)


def kernel(
    grads, owner, roster, left_stats, right_stats, left_root, right_root,
    updates, out_sl, out_sr, out_rl, out_rr,
    own, peer, b1p, b1m, b2p, b2m, fin, snd, rcv, grad,
    st, keep, mat, fac, cur, upd, turn, back, res, idx,
    own_sem, in_sem, core_s, core_r, z_s, z_r, pl_s, pl_r, dp_s, dp_r,
    h1_s, h1_r, h2_s, h2_r, out_sem,
):
    d = lax.axis_index("dp")
    h = lax.axis_index("fsdp")
    z = d // 2
    core = d % 2
    up = (z + 1) % NZ
    down = (z + 3) % NZ
    far = (z + 2) % NZ

    def at_dp(x):
        return {"dp": x, "fsdp": h}

    def at_fsdp(x):
        return {"dp": d, "fsdp": x}

    def own_copy(r):
        return pltpu.make_async_copy(grads.at[:, :, core, r], own.at[r], own_sem.at[r])

    def remote(src, dst, s, r, dev):
        return pltpu.make_async_remote_copy(
            src_ref=src, dst_ref=dst, send_sem=s, recv_sem=r, device_id=dev, device_id_type=MESH
        )

    def core_copy(r):
        return remote(grads.at[:, :, 1 - core, r], peer.at[r], core_s.at[r], core_r.at[r], at_dp(2 * z + 1 - core))

    dev_up = at_dp(2 * up + core)
    dev_down = at_dp(2 * down + core)
    lo = pl.ds(0, HALF)
    hi = pl.ds(HALF, HALF)

    def z_copy(kind, r):
        if kind == 0:
            src, dst, dev = own.at[r, lo, far], b1p.at[r], dev_up
        elif kind == 1:
            src, dst, dev = own.at[r, hi, far], b1m.at[r], dev_down
        elif kind == 2:
            src, dst, dev = own.at[r, hi, up], b2p.at[r, hi], dev_up
        elif kind == 3:
            src, dst, dev = own.at[r, lo, down], b2m.at[r, lo], dev_down
        elif kind == 4:
            src, dst, dev = own.at[r, lo, up], b2p.at[r, lo], dev_up
        else:
            src, dst, dev = own.at[r, hi, down], b2m.at[r, hi], dev_down
        return remote(src, dst, z_s.at[kind, r], z_r.at[kind, r], dev)

    def plane_send(r, o):
        return remote(snd.at[r, o], rcv.at[r, h], pl_s.at[r, o], pl_r.at[r, h], at_fsdp(o))

    def plane_recv(r, o):
        return remote(snd.at[r, o], rcv.at[r, o], pl_s.at[r, o], pl_r.at[r, o], at_fsdp(o))

    def rows_of(x, r):
        return pl.ds(pl.multiple_of(x * ROWS + r * RR, RR), RR)

    def dp_send(r, x):
        return remote(
            rcv.at[r, pl.ds(2 * x, 2)], grad.at[:, rows_of(d, r)], dp_s.at[r, x], dp_r.at[r, d], at_dp(x)
        )

    def dp_recv(r, x):
        return remote(
            rcv.at[r, pl.ds(2 * x, 2)], grad.at[:, rows_of(x, r)], dp_s.at[r, x], dp_r.at[r, x], at_dp(x)
        )

    def chunk(x):
        return pl.ds(pl.multiple_of(x * ROWS, ROWS), ROWS)

    def h1_send(j, x):
        return remote(upd.at[j, chunk(x)], turn.at[2 * d + j], h1_s.at[j, x], h1_r.at[2 * d + j], at_dp(x))

    def h1_recv(g, x):
        return remote(upd.at[0, chunk(x)], turn.at[g], h1_s.at[0, x], h1_r.at[g], at_dp(x))

    def h2_send(g):
        return remote(turn.at[g], back.at[h], h2_s.at[g], h2_r.at[h], at_fsdp(g))

    def h2_recv(o):
        return remote(turn.at[o], back.at[o], h2_s.at[o], h2_r.at[o], at_fsdp(o))

    def stat_in(i):
        return pltpu.make_async_copy((left_stats, right_stats)[i], st.at[i], in_sem.at[i])

    def keep_in(i):
        return pltpu.make_async_copy((left_root, right_root)[i], keep.at[i], in_sem.at[2 + i])

    def stat_out(i, j):
        return pltpu.make_async_copy(st.at[i, j], (out_sl, out_sr)[i].at[j], out_sem.at[i, j])

    def root_out(i, j):
        return pltpu.make_async_copy(keep.at[i, j], (out_rl, out_rr)[i].at[j], out_sem.at[2 + i, j])

    own_copy(0).start()
    for i in range(2):
        stat_in(i).start()
    for r in range(1, R):
        own_copy(r).start()
    for i in range(2):
        keep_in(i).start()

    barrier = pltpu.get_barrier_semaphore()

    @pl.loop(1, N_DP)
    def _(i):
        pl.semaphore_signal(barrier, inc=1, device_id=at_dp((d + i) % N_DP), device_id_type=MESH)

    @pl.loop(1, N_FSDP)
    def _(i):
        pl.semaphore_signal(barrier, inc=1, device_id=at_fsdp((h + i) % N_FSDP), device_id_type=MESH)

    pl.semaphore_wait(barrier, N_DP + N_FSDP - 2)

    @pl.loop(0, R)
    def _(r):
        core_copy(r).start()

    @pl.loop(0, N_FSDP)
    def _(o):
        place = jnp.int32(HOMEB)
        for k in range(HOMEB):
            place = jnp.where(owner[h * HOMEB + k] == o, jnp.int32(k), place)
        idx[o] = place

    fin[HOMEB] = jnp.zeros((RR, BS), BF)
    for i in range(2):
        stat_in(i).wait()
    for i in range(2):
        keep_in(i).wait()

    ii = lax.broadcasted_iota(jnp.int32, (BS, BS), 0)
    jj = lax.broadcasted_iota(jnp.int32, (BS, BS), 1)

    def factor(m):
        return (jnp.where(ii == jj, 1.25, 0.0) - 0.25 * m).astype(BF)

    def root_step(t):
        slot = t // 3
        sweep = t % 3

        @pl.when(sweep == 0)
        def _():
            for i in range(2):
                a = st[i, slot]
                bound = jnp.max(jnp.sum(jnp.abs(a), axis=0, keepdims=True), axis=1, keepdims=True)
                m = a * (1.0 / bound)
                f = factor(m)
                mat[i] = m.astype(BF)
                fac[i] = f
                first = lax.rsqrt(jnp.sqrt(bound)).astype(BF).astype(F32)
                cur[i] = (first * f.astype(F32)).astype(BF)

        for i in range(2):
            f = fac[i]
            f2 = dot(f, f).astype(BF)
            f4 = dot(f2, f2).astype(BF)
            m = dot(f4, mat[i])
            mat[i] = m.astype(BF)
            f = factor(m)
            fac[i] = f
            cur[i] = dot(cur[i], f).astype(BF)

        @pl.when(sweep == 2)
        def _():
            flag = jnp.int32(0)
            for k in range(HOMEB):
                spot = (2 * d + slot) * HOMEB + k
                flag += jnp.where(owner[spot] == h, roster[spot], 0)
            for i in range(2):
                keep[i, slot] = jnp.where(flag > 0, cur[i], keep[i, slot])

    def stage_a(r):
        own_copy(r).wait()
        core_copy(r).wait_recv()

        @pl.loop(0, HOMEB)
        def _(k):
            own[r, k] = (own[r, k].astype(F32) + peer[r, k].astype(F32)).astype(BF)

        for kind in range(4):
            z_copy(kind, r).start()

    def stage_b(r):
        z_copy(0, r).wait_recv()
        own[r, lo, up] = (own[r, lo, up].astype(F32) + b1p[r].astype(F32)).astype(BF)
        z_copy(4, r).start()
        z_copy(1, r).wait_recv()
        own[r, hi, down] = (own[r, hi, down].astype(F32) + b1m[r].astype(F32)).astype(BF)
        z_copy(5, r).start()

    def stage_c(r):
        for kind in range(2, 6):
            z_copy(kind, r).wait_recv()

        fin[pl.ds(0, HOMEB)] = (
            own[r, :, z].astype(F32) + b2p[r].astype(F32) + b2m[r].astype(F32)
        ).astype(BF)

        @pl.loop(0, N_FSDP)
        def _(o):
            snd[r, o] = fin[idx[o]]

        rcv[r, h] = snd[r, h]

        @pl.loop(1, N_FSDP)
        def _(i):
            plane_send(r, (h + i) % N_FSDP).start()

    def stage_d(r):
        @pl.loop(1, N_FSDP)
        def _(i):
            plane_recv(r, (h + i) % N_FSDP).wait_recv()

        grad[:, rows_of(d, r)] = rcv[r, pl.ds(2 * d, 2)]

        @pl.loop(1, N_DP)
        def _(i):
            dp_send(r, (d + i) % N_DP).start()

    @pl.loop(0, R + 3)
    def _(t):
        @pl.when(t < R)
        def _():
            stage_a(t)

        @pl.when(jnp.logical_and(t >= 1, t < R + 1))
        def _():
            stage_b(t - 1)

        @pl.when(jnp.logical_and(t >= 2, t < R + 2))
        def _():
            stage_c(t - 2)

        @pl.when(t >= 3)
        def _():
            stage_d(t - 3)

        @pl.when(t < ROOT_STEPS)
        def _():
            root_step(t)

    for i in range(2):
        for j in range(2):
            root_out(i, j).start()

    @pl.loop(0, R)
    def _(r):
        @pl.loop(1, N_DP)
        def _(i):
            dp_recv(r, (d + i) % N_DP).wait_recv()

    @pl.loop(0, 2)
    def _(j):
        g = grad[j]
        half = dot(keep[0, j], g).astype(BF)
        direction = dot(half, keep[1, j])
        g = g.astype(F32)
        count = float(BS * BS)
        grad_sq = jnp.sum(jnp.sum(g * g, axis=0, keepdims=True), axis=1, keepdims=True)
        dir_sq = jnp.sum(jnp.sum(direction * direction, axis=0, keepdims=True), axis=1, keepdims=True)
        ratio = jnp.sqrt(grad_sq / count) / jnp.sqrt(dir_sq / count + 1e-06)
        upd[j] = (-learn_rate * direction * ratio).astype(BF)
        turn[2 * d + j] = upd[j, chunk(d)]

        @pl.loop(1, N_DP)
        def _(i):
            h1_send(j, (d + i) % N_DP).start()

    def forward(i, j):
        x = (d + i) % N_DP
        g = 2 * x + j

        @pl.when(i > 0)
        def _():
            h1_recv(g, x).wait_recv()

        @pl.when(g != h)
        def _():
            h2_send(g).start()

        @pl.when(g == h)
        def _():
            back[h] = turn[h]

    @pl.loop(0, 2)
    def _(j):
        @pl.loop(0, N_DP)
        def _(i):
            forward(i, j)

    @pl.loop(0, 2)
    def _(j):
        g = grad[j]
        st[0, j] = decay_rate * st[0, j] + (1.0 - decay_rate) * dot(g, g, 1, 1)
        st[1, j] = decay_rate * st[1, j] + (1.0 - decay_rate) * dot(g, g, 0, 0)

    for i in range(2):
        for j in range(2):
            stat_out(i, j).start()

    @pl.loop(1, N_FSDP)
    def _(i):
        h2_recv((h + i) % N_FSDP).wait_recv()

    @pl.loop(0, HOMEB)
    def _(k):
        res[k] = back[owner[h * HOMEB + k]]

    last = pltpu.make_async_copy(res, updates, out_sem.at[4, 0])
    last.start()

    @pl.loop(0, R)
    def _(r):
        core_copy(r).wait_send()
        for kind in range(6):
            z_copy(kind, r).wait_send()

        @pl.loop(1, N_FSDP)
        def _(i):
            plane_send(r, (h + i) % N_FSDP).wait_send()

        @pl.loop(1, N_DP)
        def _(i):
            dp_send(r, (d + i) % N_DP).wait_send()

    @pl.loop(1, N_DP)
    def _(i):
        for j in range(2):
            h1_send(j, (d + i) % N_DP).wait_send()

    @pl.loop(1, N_FSDP)
    def _(i):
        h2_send((h + i) % N_FSDP).wait_send()

    for i in range(2):
        for j in range(2):
            root_out(i, j).wait()
            stat_out(i, j).wait()
    last.wait()


def local(grads, owner, roster, left_stats, right_stats, left_root, right_root):
    anywhere = pl.BlockSpec(memory_space=pl.ANY)
    scalars = pl.BlockSpec(memory_space=pltpu.SMEM)
    dma = pltpu.SemaphoreType.DMA
    shape = jax.ShapeDtypeStruct
    outs = pl.pallas_call(
        kernel,
        out_shape=(
            shape((HOMEB, ROWS, BS), BF),
            shape((2, BS, BS), F32),
            shape((2, BS, BS), F32),
            shape((2, BS, BS), BF),
            shape((2, BS, BS), BF),
        ),
        in_specs=[anywhere, scalars, scalars] + [anywhere] * 4,
        out_specs=[anywhere] * 5,
        scratch_shapes=[
            pltpu.VMEM((R, HOMEB, NZ, RR, BS), BF),
            pltpu.VMEM((R, HOMEB, NZ, RR, BS), BF),
            pltpu.VMEM((R, HALF, RR, BS), BF),
            pltpu.VMEM((R, HALF, RR, BS), BF),
            pltpu.VMEM((R, HOMEB, RR, BS), BF),
            pltpu.VMEM((R, HOMEB, RR, BS), BF),
            pltpu.VMEM((HOMEB + 1, RR, BS), BF),
            pltpu.VMEM((R, N_FSDP, RR, BS), BF),
            pltpu.VMEM((R, N_FSDP, RR, BS), BF),
            pltpu.VMEM((2, BS, BS), BF),
            pltpu.VMEM((2, 2, BS, BS), F32),
            pltpu.VMEM((2, 2, BS, BS), BF),
            pltpu.VMEM((2, BS, BS), BF),
            pltpu.VMEM((2, BS, BS), BF),
            pltpu.VMEM((2, BS, BS), BF),
            pltpu.VMEM((2, BS, BS), BF),
            pltpu.VMEM((N_FSDP, ROWS, BS), BF),
            pltpu.VMEM((N_FSDP, ROWS, BS), BF),
            pltpu.VMEM((HOMEB, ROWS, BS), BF),
            pltpu.SMEM((N_FSDP,), jnp.int32),
            dma((R,)),
            dma((4,)),
            dma((R,)),
            dma((R,)),
            dma((6, R)),
            dma((6, R)),
            dma((R, N_FSDP)),
            dma((R, N_FSDP)),
            dma((R, N_DP)),
            dma((R, N_DP)),
            dma((2, N_DP)),
            dma((N_FSDP,)),
            dma((N_FSDP,)),
            dma((N_FSDP,)),
            dma((5, 2)),
        ],
        compiler_params=pltpu.CompilerParams(
            collective_id=0, has_side_effects=True, vmem_limit_bytes=56 * 1024 * 1024
        ),
        cost_estimate=pl.CostEstimate(flops=16 * 10**9, bytes_accessed=24 * 10**6, transcendentals=0),
        name="shampoo",
    )(
        grads.reshape(HOMEB, NZ, 2, R, RR, BS),
        owner,
        roster,
        left_stats[0, 0],
        right_stats[0, 0],
        left_root[0, 0],
        right_root[0, 0],
    )
    result, new_left, new_right, roots_left, roots_right = outs
    return (result, new_left[None, None], new_right[None, None], roots_left[None, None], roots_right[None, None])


def solution(mesh):
    placed = P("dp", "fsdp", None, None, None)
    return jax.shard_map(
        local,
        mesh=mesh,
        in_specs=(P("dp", "fsdp", None, None), P(), P(), placed, placed, placed, placed),
        out_specs=(P("fsdp", "dp", None), placed, placed, placed, placed),
        check_vma=False,
    )
```

```python
import functools

import jax
import jax.numpy as jnp
from jax import lax
from jax.experimental import pallas as pl
from jax.experimental.pallas import tpu as pltpu
from jax.sharding import PartitionSpec as P

BS = 512
HOMEB = 14
HALF = HOMEB // 2
NZ = 4
N_DP = 8
N_FSDP = 16
ROWS = BS // N_DP
R = 4
RR = ROWS // R
LAST = R - 1
ROOT_STEPS = 6
STEPS = 9
PIECES = 2
PIECE = ROWS // PIECES
decay_rate = 0.9
learn_rate = 10.0
BF = jnp.bfloat16
F32 = jnp.float32
MESH = pl.DeviceIdType.MESH


def dot(a, b, ca=1, cb=0):
    return lax.dot_general(a, b, (((ca,), (cb,)), ((), ())), preferred_element_type=F32)


def kernel(
    grads, owner_in, roster_in, left_stats, right_stats, left_root, right_root,
    res, st, keep,
    own, peer, mix, b1p, b1m, b2p, b2m, fin, snd, rcv, grad,
    mat, fac, cur, upd, turn, back, idx, owner, roster,
    own_sem, in_sem, core_s, core_r, x_s, x_r, z_s, z_r, pl_s, pl_r, dp_s, dp_r, ex_s, ex_r,
    h1_s, h1_r, h2_s, h2_r,
):
    d = lax.axis_index("dp")
    h = lax.axis_index("fsdp")
    z = d // 2
    core = d % 2
    x = h // 4
    y = h % 4
    up = (z + 1) % NZ
    down = (z + 3) % NZ
    far = (z + 2) % NZ

    def at_dp(x):
        return {"dp": x, "fsdp": h}

    def at_fsdp(x):
        return {"dp": d, "fsdp": x}

    def own_copy(r):
        return pltpu.make_async_copy(grads.at[:, :, core, r], own.at[r], own_sem.at[r])

    def remote(src, dst, s, r, dev):
        return pltpu.make_async_remote_copy(
            src_ref=src, dst_ref=dst, send_sem=s, recv_sem=r, device_id=dev, device_id_type=MESH
        )

    def core_copy(r):
        return remote(grads.at[:, :, 1 - core, r], peer.at[r], core_s.at[r], core_r.at[r], at_dp(2 * z + 1 - core))

    dev_up = at_dp(2 * up + core)
    dev_down = at_dp(2 * down + core)
    lo = pl.ds(0, HALF)
    hi = pl.ds(HALF, HALF)

    def held(r, mixed):
        return mix if mixed else own.at[r]

    def z_copy(kind, r, mixed):
        part = held(r, mixed)
        if kind == 0:
            src, dst, dev = part.at[lo, far], b1p.at[r], dev_up
        elif kind == 1:
            src, dst, dev = part.at[hi, far], b1m.at[r], dev_down
        elif kind == 2:
            src, dst, dev = part.at[hi, up], b2p.at[r, hi], dev_up
        elif kind == 3:
            src, dst, dev = part.at[lo, down], b2m.at[r, lo], dev_down
        elif kind == 4:
            src, dst, dev = part.at[lo, up], b2p.at[r, lo], dev_up
        else:
            src, dst, dev = part.at[hi, down], b2m.at[r, hi], dev_down
        return remote(src, dst, z_s.at[kind, r], z_r.at[kind, r], dev)

    def x_send(i):
        q = (x + i) % 4
        return remote(own.at[LAST, :, q], mix.at[:, x], x_s.at[q], x_r.at[x], at_fsdp(4 * q + y))

    def x_recv(i):
        q = (x + i) % 4
        return remote(own.at[LAST, :, q], mix.at[:, q], x_s.at[q], x_r.at[q], at_fsdp(4 * q + y))

    def plane_send(r, o):
        return remote(snd.at[r, o], rcv.at[r, h], pl_s.at[r, o], pl_r.at[r, h], at_fsdp(o))

    def plane_recv(r, o):
        return remote(snd.at[r, o], rcv.at[r, o], pl_s.at[r, o], pl_r.at[r, o], at_fsdp(o))

    def rows_of(x, r):
        return pl.ds(pl.multiple_of(x * ROWS + r * RR, RR), RR)

    def dp_send(r, x):
        return remote(
            rcv.at[r, pl.ds(2 * x, 2)], grad.at[:, rows_of(d, r)], dp_s.at[r, x], dp_r.at[r, d], at_dp(x)
        )

    def dp_recv(r, x):
        return remote(
            rcv.at[r, pl.ds(2 * x, 2)], grad.at[:, rows_of(x, r)], dp_s.at[r, x], dp_r.at[r, x], at_dp(x)
        )

    def ex_send(o):
        return remote(
            snd.at[LAST, o], grad.at[y % 2, rows_of(2 * x + core, LAST)],
            ex_s.at[o], ex_r.at[(y % 2) * N_DP + 2 * x + core],
            {"dp": 2 * z + y // 2, "fsdp": o},
        )

    def ex_recv(i):
        return remote(
            snd.at[LAST, 0], grad.at[i // N_DP, rows_of(i % N_DP, LAST)], ex_s.at[0], ex_r.at[i],
            {"dp": d, "fsdp": (h + 1) % N_FSDP},
        )

    def chunk(x):
        return pl.ds(pl.multiple_of(x * ROWS, ROWS), ROWS)

    def piece(x, p):
        return pl.ds(pl.multiple_of(x * ROWS + p * PIECE, PIECE), PIECE)

    def h1_send(j, p, x):
        return remote(
            upd.at[j, piece(x, p)], turn.at[2 * d + j, p], h1_s.at[j, p, x], h1_r.at[2 * d + j, p], at_dp(x)
        )

    def h1_recv(g, p, x):
        return remote(upd.at[0, piece(x, p)], turn.at[g, p], h1_s.at[0, p, x], h1_r.at[g, p], at_dp(x))

    def h2_send(g, p):
        return remote(turn.at[g, p], back.at[h, p], h2_s.at[g, p], h2_r.at[h, p], at_fsdp(g))

    def h2_recv(o, p):
        return remote(turn.at[o, p], back.at[o, p], h2_s.at[o, p], h2_r.at[o, p], at_fsdp(o))

    def stat_in(i):
        return pltpu.make_async_copy((left_stats, right_stats)[i], st.at[i], in_sem.at[i])

    def keep_in(i):
        return pltpu.make_async_copy((left_root, right_root)[i], keep.at[i], in_sem.at[2 + i])

    tables = [
        pltpu.make_async_copy(owner_in, owner, in_sem.at[4]),
        pltpu.make_async_copy(roster_in, roster, in_sem.at[5]),
    ]
    for table in tables:
        table.start()

    @pl.loop(0, R)
    def _(r):
        own_copy(r).start()

    barrier = pltpu.get_barrier_semaphore()

    @pl.loop(1, N_DP)
    def _(i):
        pl.semaphore_signal(barrier, inc=1, device_id=at_dp((d + i) % N_DP), device_id_type=MESH)

    @pl.loop(1, N_FSDP)
    def _(i):
        pl.semaphore_signal(barrier, inc=1, device_id=at_fsdp((h + i) % N_FSDP), device_id_type=MESH)

    @pl.loop(0, N_DP)
    def _(i):
        there = {"dp": 2 * z + 1 - core, "fsdp": (i // 2) * 4 + 2 * core + i % 2}
        pl.semaphore_signal(barrier, inc=1, device_id=there, device_id_type=MESH)

    pl.semaphore_wait(barrier, N_DP + N_FSDP - 2 + jnp.where(y // 2 == core, 0, N_FSDP))

    core_copy(0).start()
    core_copy(LAST).start()

    def begin():
        for i in range(2):
            stat_in(i).start()
        for i in range(2):
            keep_in(i).start()

        for table in tables:
            table.wait()

        @pl.loop(0, N_FSDP)
        def _(o):
            for i, home in enumerate((h, 4 * z + y)):
                place = jnp.int32(HOMEB)
                for k in range(HOMEB):
                    place = jnp.where(owner[home * HOMEB + k] == o, jnp.int32(k), place)
                idx[i, o] = place

        fin[HOMEB] = jnp.zeros((RR, BS), BF)
        for i in range(2):
            stat_in(i).wait()
        for i in range(2):
            keep_in(i).wait()

    ii = lax.broadcasted_iota(jnp.int32, (BS, BS), 0)
    jj = lax.broadcasted_iota(jnp.int32, (BS, BS), 1)

    def factor(m):
        return (jnp.where(ii == jj, 1.25, 0.0) - 0.25 * m).astype(BF)

    def root_step(t):
        slot = t // 3
        sweep = t % 3

        @pl.when(sweep == 0)
        def _():
            for i in range(2):
                a = st[i, slot]
                bound = jnp.max(jnp.sum(jnp.abs(a), axis=0, keepdims=True), axis=1, keepdims=True)
                m = a * (1.0 / bound)
                f = factor(m)
                mat[i] = m.astype(BF)
                fac[i] = f
                first = lax.rsqrt(jnp.sqrt(bound)).astype(BF).astype(F32)
                cur[i] = (first * f.astype(F32)).astype(BF)

        for i in range(2):
            f = fac[i]
            f2 = dot(f, f).astype(BF)
            f4 = dot(f2, f2).astype(BF)
            m = dot(f4, mat[i])
            mat[i] = m.astype(BF)
            f = factor(m)
            fac[i] = f
            cur[i] = dot(cur[i], f).astype(BF)

        @pl.when(sweep == 2)
        def _():
            flag = jnp.int32(0)
            for k in range(HOMEB):
                spot = (2 * d + slot) * HOMEB + k
                flag += jnp.where(owner[spot] == h, roster[spot], 0)
            for i in range(2):
                keep[i, slot] = jnp.where(flag > 0, cur[i], keep[i, slot])

    def stage_a(r):
        own_copy(r).wait()
        core_copy(r).wait_recv()

        @pl.when(r == 0)
        def _():
            core_copy(1).start()

        @pl.when(r == LAST)
        def _():
            core_copy(2).start()

        @pl.loop(0, HOMEB)
        def _(k):
            own[r, k] = own[r, k] + peer[r, k]

    def begin_z(r, mixed):
        for kind in range(2):
            z_copy(kind, r, mixed).start()

        @pl.when(r != LAST)
        def _():
            for kind in range(2, 4):
                z_copy(kind, r, mixed).start()

    def begin_x():
        for i in (2, 1, 3):
            x_send(i).start()
        mix[:, x] = own[LAST, :, x]

    def end_x():
        for i in (2, 1, 3):
            x_recv(i).wait_recv()
        begin_z(LAST, True)

    def stage_b(r, mixed):
        part = held(r, mixed)
        z_copy(0, r, mixed).wait_recv()
        part[lo, up] = part[lo, up] + b1p[r]
        z_copy(4, r, mixed).start()
        z_copy(1, r, mixed).wait_recv()
        part[hi, down] = part[hi, down] + b1m[r]
        z_copy(5, r, mixed).start()

        @pl.when(r == LAST)
        def _():
            for kind in range(2, 4):
                z_copy(kind, r, mixed).start()

    def stage_c(r, mixed):
        part = held(r, mixed)
        for kind in range(2, 6):
            z_copy(kind, r, mixed).wait_recv()

        fin[pl.ds(0, HOMEB)] = (
            part[:, z].astype(F32) + b2p[r].astype(F32) + b2m[r].astype(F32)
        ).astype(BF)

        @pl.loop(0, N_FSDP)
        def _(o):
            snd[r, o] = fin[idx[1 if mixed else 0, o]]

        if mixed:
            @pl.loop(1, N_FSDP)
            def _(i):
                ex_send((h + 5 * i) % N_FSDP).start()

            @pl.when(y // 2 != core)
            def _():
                ex_send(h).start()

            @pl.when(y // 2 == core)
            def _():
                grad[y % 2, rows_of(2 * x + core, r)] = snd[r, h]
        else:
            rcv[r, h] = snd[r, h]

            @pl.loop(1, N_FSDP)
            def _(i):
                plane_send(r, (h + 5 * i) % N_FSDP).start()

    def stage_d(r):
        @pl.loop(1, N_FSDP)
        def _(i):
            plane_recv(r, (h + i) % N_FSDP).wait_recv()

        grad[:, rows_of(d, r)] = rcv[r, pl.ds(2 * d, 2)]

        @pl.loop(1, N_DP)
        def _(i):
            dp_send(r, (d + 3 * i) % N_DP).start()

    def either(t, *steps):
        return functools.reduce(jnp.logical_or, [t == step for step in steps])

    @pl.loop(0, STEPS)
    def _(t):
        @pl.when(t < R)
        def _():
            stage_a(jnp.where(t == 1, LAST, jnp.maximum(t - 1, 0)))

        @pl.when(either(t, 0, 2, 3))
        def _():
            begin_z(jnp.maximum(t - 1, 0), False)

        @pl.when(t == 1)
        def _():
            begin_x()

        @pl.when(t == 2)
        def _():
            begin()

        @pl.when(either(t, 2, 3, 4))
        def _():
            stage_b(t - 2, False)

        @pl.when(t == 5)
        def _():
            end_x()

        @pl.when(t == 6)
        def _():
            stage_b(LAST, True)

        @pl.when(either(t, 4, 5, 6))
        def _():
            stage_c(t - 4, False)

        @pl.when(either(t, 5, 6, 7))
        def _():
            stage_d(t - 5)

        @pl.when(t == 8)
        def _():
            stage_c(LAST, True)

        @pl.when(jnp.logical_and(t >= 2, t < 2 + ROOT_STEPS))
        def _():
            root_step(t - 2)

    def from_me(i):
        return jnp.logical_and(i == (y % 2) * N_DP + 2 * x + core, y // 2 == core)

    @pl.loop(0, LAST)
    def _(r):
        @pl.loop(1, N_DP)
        def _(i):
            dp_recv(r, (d + i) % N_DP).wait_recv()

    @pl.loop(0, 2 * N_DP)
    def _(i):
        @pl.when(jnp.logical_not(from_me(i)))
        def _():
            ex_recv(i).wait_recv()

    @pl.loop(0, 2)
    def _(j):
        g = grad[j]
        half = dot(keep[0, j], g).astype(BF)
        direction = dot(half, keep[1, j])
        g = g.astype(F32)
        count = float(BS * BS)
        grad_sq = jnp.sum(jnp.sum(g * g, axis=0, keepdims=True), axis=1, keepdims=True)
        dir_sq = jnp.sum(jnp.sum(direction * direction, axis=0, keepdims=True), axis=1, keepdims=True)
        ratio = jnp.sqrt(grad_sq / count) / jnp.sqrt(dir_sq / count + 1e-06)
        upd[j] = (-learn_rate * direction * ratio).astype(BF)
        for p in range(PIECES):
            turn[2 * d + j, p] = upd[j, piece(d, p)]

            @pl.loop(1, N_DP)
            def _(i):
                h1_send(j, p, (d + 3 * i) % N_DP).start()

    def forward(i, j, p):
        x = (d + 5 * i) % N_DP
        g = 2 * x + j

        @pl.when(i > 0)
        def _():
            h1_recv(g, p, x).wait_recv()

        @pl.when(g != h)
        def _():
            h2_send(g, p).start()

        @pl.when(g == h)
        def _():
            back[h, p] = turn[h, p]

    @pl.loop(0, 2)
    def _(j):
        @pl.loop(0, PIECES)
        def _(p):
            @pl.loop(0, N_DP)
            def _(i):
                forward(i, j, p)

    @pl.loop(0, 2)
    def _(j):
        g = grad[j]
        st[0, j] = decay_rate * st[0, j] + (1.0 - decay_rate) * dot(g, g, 1, 1)
        st[1, j] = decay_rate * st[1, j] + (1.0 - decay_rate) * dot(g, g, 0, 0)

    @pl.loop(1, N_FSDP)
    def _(i):
        for p in range(PIECES):
            h2_recv((h + i) % N_FSDP, p).wait_recv()

    @pl.loop(0, HOMEB)
    def _(k):
        for p in range(PIECES):
            res[k, pl.ds(p * PIECE, PIECE)] = back[owner[h * HOMEB + k], p]

    @pl.loop(0, R)
    def _(r):
        core_copy(r).wait_send()
        for kind in range(6):
            z_copy(kind, r, False).wait_send()

    for i in (1, 2, 3):
        x_send(i).wait_send()

    @pl.loop(0, LAST)
    def _(r):
        @pl.loop(1, N_FSDP)
        def _(i):
            plane_send(r, (h + i) % N_FSDP).wait_send()

        @pl.loop(1, N_DP)
        def _(i):
            dp_send(r, (d + i) % N_DP).wait_send()

    @pl.loop(1, N_FSDP)
    def _(i):
        ex_send((h + i) % N_FSDP).wait_send()

    @pl.when(y // 2 != core)
    def _():
        ex_send(h).wait_send()

    @pl.loop(0, PIECES)
    def _(p):
        @pl.loop(1, N_DP)
        def _(i):
            for j in range(2):
                h1_send(j, p, (d + i) % N_DP).wait_send()

        @pl.loop(1, N_FSDP)
        def _(i):
            h2_send((h + i) % N_FSDP, p).wait_send()


def finish(res, st, keep, updates, out_sl, out_sr, out_rl, out_rr, sem):
    copies = [pltpu.make_async_copy(res, updates, sem.at[8])]
    for i in range(2):
        for j in range(2):
            copies.append(pltpu.make_async_copy(st.at[i, j], (out_sl, out_sr)[i].at[j], sem.at[2 * i + j]))
            copies.append(pltpu.make_async_copy(keep.at[i, j], (out_rl, out_rr)[i].at[j], sem.at[4 + 2 * i + j]))
    for copy in copies:
        copy.start()
    for copy in copies:
        copy.wait()


def local(grads, owner, roster, left_stats, right_stats, left_root, right_root):
    anywhere = pl.BlockSpec(memory_space=pl.ANY)
    dma = pltpu.SemaphoreType.DMA
    shape = jax.ShapeDtypeStruct
    outs = pl.pallas_call(
        kernel,
        out_shape=(
            pltpu.VMEM((HOMEB, ROWS, BS), BF),
            pltpu.VMEM((2, 2, BS, BS), F32),
            pltpu.VMEM((2, 2, BS, BS), BF),
        ),
        in_specs=[anywhere] * 7,
        out_specs=[pl.BlockSpec(memory_space=pltpu.VMEM)] * 3,
        scratch_shapes=[
            pltpu.VMEM((R, HOMEB, NZ, RR, BS), BF),
            pltpu.VMEM((R, HOMEB, NZ, RR, BS), BF),
            pltpu.VMEM((HOMEB, NZ, RR, BS), BF),
            pltpu.VMEM((R, HALF, RR, BS), BF),
            pltpu.VMEM((R, HALF, RR, BS), BF),
            pltpu.VMEM((R, HOMEB, RR, BS), BF),
            pltpu.VMEM((R, HOMEB, RR, BS), BF),
            pltpu.VMEM((HOMEB + 1, RR, BS), BF),
            pltpu.VMEM((R, N_FSDP, RR, BS), BF),
            pltpu.VMEM((R, N_FSDP, RR, BS), BF),
            pltpu.VMEM((2, BS, BS), BF),
            pltpu.VMEM((2, BS, BS), BF),
            pltpu.VMEM((2, BS, BS), BF),
            pltpu.VMEM((2, BS, BS), BF),
            pltpu.VMEM((2, BS, BS), BF),
            pltpu.VMEM((N_FSDP, PIECES, PIECE, BS), BF),
            pltpu.VMEM((N_FSDP, PIECES, PIECE, BS), BF),
            pltpu.SMEM((2, N_FSDP), jnp.int32),
            pltpu.SMEM((N_FSDP * HOMEB,), jnp.int32),
            pltpu.SMEM((N_FSDP * HOMEB,), jnp.int32),
            dma((R,)),
            dma((6,)),
            dma((R,)),
            dma((R,)),
            dma((4,)),
            dma((4,)),
            dma((6, R)),
            dma((6, R)),
            dma((R, N_FSDP)),
            dma((R, N_FSDP)),
            dma((R, N_DP)),
            dma((R, N_DP)),
            dma((N_FSDP,)),
            dma((N_FSDP,)),
            dma((2, PIECES, N_DP)),
            dma((N_FSDP, PIECES)),
            dma((N_FSDP, PIECES)),
            dma((N_FSDP, PIECES)),
        ],
        compiler_params=pltpu.CompilerParams(
            collective_id=0, has_side_effects=True, vmem_limit_bytes=40 * 1024 * 1024
        ),
        cost_estimate=pl.CostEstimate(flops=16 * 10**9, bytes_accessed=24 * 10**6, transcendentals=0),
        name="shampoo",
    )(
        *[
            pltpu.with_memory_space_constraint(array, pltpu.HBM)
            for array in (
                grads.reshape(HOMEB, NZ, 2, R, RR, BS), owner, roster,
                left_stats[0, 0], right_stats[0, 0], left_root[0, 0], right_root[0, 0],
            )
        ],
    )
    result, new_left, new_right, roots_left, roots_right = pl.pallas_call(
        finish,
        out_shape=(
            shape((HOMEB, ROWS, BS), BF),
            shape((2, BS, BS), F32),
            shape((2, BS, BS), F32),
            shape((2, BS, BS), BF),
            shape((2, BS, BS), BF),
        ),
        in_specs=[anywhere] * 3,
        out_specs=[anywhere] * 5,
        scratch_shapes=[dma((9,))],
        compiler_params=pltpu.CompilerParams(vmem_limit_bytes=2 * 1024 * 1024),
        name="finish",
    )(*[pltpu.with_memory_space_constraint(out, pltpu.VMEM) for out in outs])
    return (result, new_left[None, None], new_right[None, None], roots_left[None, None], roots_right[None, None])


def solution(mesh):
    placed = P("dp", "fsdp", None, None, None)
    return jax.shard_map(
        local,
        mesh=mesh,
        in_specs=(P("dp", "fsdp", None, None), P(), P(), placed, placed, placed, placed),
        out_specs=(P("fsdp", "dp", None), placed, placed, placed, placed),
        check_vma=False,
    )
```

```python
import functools

import jax
import jax.numpy as jnp
from jax import lax
from jax.experimental import pallas as pl
from jax.experimental.pallas import tpu as pltpu
from jax.sharding import PartitionSpec as P

BS = 512
HOMEB = 14
HALF = HOMEB // 2
NZ = 4
N_DP = 8
N_FSDP = 16
ROWS = BS // N_DP
R = 4
RR = ROWS // R
LAST = R - 1
ROOT_STEPS = 6
STEPS = 9
PIECES = 2
PIECE = ROWS // PIECES
decay_rate = 0.9
learn_rate = 10.0
BF = jnp.bfloat16
F32 = jnp.float32
MESH = pl.DeviceIdType.MESH


def dot(a, b, ca=1, cb=0):
    return lax.dot_general(a, b, (((ca,), (cb,)), ((), ())), preferred_element_type=F32)


def kernel(
    grads, owner_in, roster_in, left_stats, right_stats, left_root, right_root,
    back, st, keep,
    own, peer, mix, b1p, b1m, b2p, b2m, fin, snd, rcv, grad,
    mat, fac, cur, upd, turn, idx, owner, roster,
    own_sem, in_sem, sent, first_r, core_r, x_r, z_r, pl_r, dp_r, ex_r, h1_r, h2_r,
):
    d = lax.axis_index("dp")
    h = lax.axis_index("fsdp")
    z = d // 2
    core = d % 2
    x = h // 4
    y = h % 4
    up = (z + 1) % NZ
    down = (z + 3) % NZ
    far = (z + 2) % NZ

    def at_dp(x):
        return {"dp": x, "fsdp": h}

    def at_fsdp(x):
        return {"dp": d, "fsdp": x}

    def own_copy(r):
        return pltpu.make_async_copy(grads.at[:, :, core, r], own.at[r], own_sem.at[r])

    def remote(src, dst, s, r, dev):
        return pltpu.make_async_remote_copy(
            src_ref=src, dst_ref=dst, send_sem=s, recv_sem=r, device_id=dev, device_id_type=MESH
        )

    def core_copy(r):
        return remote(grads.at[:, :, 1 - core, r], peer.at[r], sent.at[0], core_r.at[r], at_dp(2 * z + 1 - core))

    def first_copy(i):
        q = (far, up, down, z)[i]
        return remote(
            grads.at[:, q, 1 - core, 0], peer.at[0, :, q], sent.at[0], first_r.at[i], at_dp(2 * z + 1 - core)
        )

    dev_up = at_dp(2 * up + core)
    dev_down = at_dp(2 * down + core)
    lo = pl.ds(0, HALF)
    hi = pl.ds(HALF, HALF)

    def held(r, mixed):
        return mix if mixed else own.at[r]

    def z_copy(kind, r, mixed):
        part = held(r, mixed)
        if kind == 0:
            src, dst, dev = part.at[lo, far], b1p.at[r], dev_up
        elif kind == 1:
            src, dst, dev = part.at[hi, far], b1m.at[r], dev_down
        elif kind == 2:
            src, dst, dev = part.at[hi, up], b2p.at[r, hi], dev_up
        elif kind == 3:
            src, dst, dev = part.at[lo, down], b2m.at[r, lo], dev_down
        elif kind == 4:
            src, dst, dev = part.at[lo, up], b2p.at[r, lo], dev_up
        else:
            src, dst, dev = part.at[hi, down], b2m.at[r, hi], dev_down
        return remote(src, dst, sent.at[1], z_r.at[min(kind, 2), r], dev)

    def x_send(i):
        q = (x + i) % 4
        return remote(own.at[LAST, :, q], mix.at[:, x], sent.at[2], x_r, at_fsdp(4 * q + y))

    def arrived(ref, semaphore):
        remote(ref, ref, sent.at[0], semaphore, dev_up).wait_recv()

    def left(ref, kind):
        remote(ref, ref, sent.at[kind], x_r, dev_up).wait_send()

    def plane_send(r, o):
        return remote(snd.at[r, o], rcv.at[r, h], sent.at[3], pl_r.at[r], at_fsdp(o))

    def rows_of(x, r):
        return pl.ds(pl.multiple_of(x * ROWS + r * RR, RR), RR)

    def dp_send(r, x):
        return remote(rcv.at[r, pl.ds(2 * x, 2)], grad.at[:, rows_of(d, r)], sent.at[4], dp_r, at_dp(x))

    def ex_send(o):
        return remote(
            snd.at[LAST, o], grad.at[y % 2, rows_of(2 * x + core, LAST)], sent.at[5], ex_r,
            {"dp": 2 * z + y // 2, "fsdp": o},
        )

    def chunk(x):
        return pl.ds(pl.multiple_of(x * ROWS, ROWS), ROWS)

    def piece(x, p):
        return pl.ds(pl.multiple_of(x * ROWS + p * PIECE, PIECE), PIECE)

    def h1_send(j, p, x):
        return remote(upd.at[j, piece(x, p)], turn.at[2 * d + j, p], sent.at[6], h1_r.at[2 * d + j, p], at_dp(x))

    def h2_send(g, p):
        return remote(turn.at[g, p], back.at[h, p], sent.at[7], h2_r, at_fsdp(g))

    def stat_in(i):
        return pltpu.make_async_copy((left_stats, right_stats)[i], st.at[i], in_sem.at[i])

    def keep_in(i):
        return pltpu.make_async_copy((left_root, right_root)[i], keep.at[i], in_sem.at[2 + i])

    tables = [
        pltpu.make_async_copy(owner_in, owner, in_sem.at[4]),
        pltpu.make_async_copy(roster_in, roster, in_sem.at[5]),
    ]
    for table in tables:
        table.start()

    @pl.loop(0, R)
    def _(r):
        own_copy(r).start()

    barrier = pltpu.get_barrier_semaphore()

    @pl.loop(0, N_DP)
    def _(i):
        there = {"dp": 2 * z + 1 - core, "fsdp": (i // 2) * 4 + 2 * core + i % 2}
        pl.semaphore_signal(barrier, inc=1, device_id=there, device_id_type=MESH)

    @pl.loop(1, N_FSDP)
    def _(i):
        pl.semaphore_signal(barrier, inc=1, device_id=at_fsdp((h + 5 * i) % N_FSDP), device_id_type=MESH)

    @pl.loop(1, N_DP)
    def _(i):
        pl.semaphore_signal(barrier, inc=1, device_id=at_dp((d + 3 * i) % N_DP), device_id_type=MESH)

    for i in range(2):
        stat_in(i).start()
    for i in range(2):
        keep_in(i).start()
    for table in tables:
        table.wait()

    @pl.loop(0, N_FSDP)
    def _(o):
        for i, home in enumerate((h, 4 * z + y)):
            place = jnp.int32(HOMEB)
            for k in range(HOMEB):
                place = jnp.where(owner[home * HOMEB + k] == o, jnp.int32(k), place)
            idx[i, o] = place

    fin[HOMEB] = jnp.zeros((RR, BS), BF)

    pl.semaphore_wait(barrier, N_DP + N_FSDP - 2 + jnp.where(y // 2 == core, 0, N_FSDP))

    for i in range(NZ):
        first_copy(i).start()
    core_copy(LAST).start()

    def begin():
        for i in range(2):
            stat_in(i).wait()
        for i in range(2):
            keep_in(i).wait()

    ii = lax.broadcasted_iota(jnp.int32, (BS, BS), 0)
    jj = lax.broadcasted_iota(jnp.int32, (BS, BS), 1)

    def factor(m):
        return (jnp.where(ii == jj, 1.25, 0.0) - 0.25 * m).astype(BF)

    def root_step(t):
        slot = t // 3
        sweep = t % 3

        @pl.when(sweep == 0)
        def _():
            for i in range(2):
                a = st[i, slot]
                bound = jnp.max(jnp.sum(jnp.abs(a), axis=0, keepdims=True), axis=1, keepdims=True)
                m = a * (1.0 / bound)
                f = factor(m)
                mat[i] = m.astype(BF)
                fac[i] = f
                first = lax.rsqrt(jnp.sqrt(bound)).astype(BF).astype(F32)
                cur[i] = (first * f.astype(F32)).astype(BF)

        for i in range(2):
            f = fac[i]
            f2 = dot(f, f).astype(BF)
            f4 = dot(f2, f2).astype(BF)
            m = dot(f4, mat[i])
            mat[i] = m.astype(BF)
            f = factor(m)
            fac[i] = f
            cur[i] = dot(cur[i], f).astype(BF)

        @pl.when(sweep == 2)
        def _():
            flag = jnp.int32(0)
            for k in range(HOMEB):
                spot = (2 * d + slot) * HOMEB + k
                flag += jnp.where(owner[spot] == h, roster[spot], 0)
            for i in range(2):
                keep[i, slot] = jnp.where(flag > 0, cur[i], keep[i, slot])

    def stage_a(r):
        own_copy(r).wait()
        core_copy(r).wait_recv()

        @pl.when(r == LAST)
        def _():
            core_copy(2).start()

        @pl.loop(0, HOMEB)
        def _(k):
            own[r, k] = own[r, k] + peer[r, k]

    def stage_a0():
        own_copy(0).wait()
        for i, q in enumerate((far, up, down, z)):
            first_copy(i).wait_recv()
            own[0, :, q] = own[0, :, q] + peer[0, :, q]
            for kind in ((0, 1), (2,), (3,), ())[i]:
                z_copy(kind, 0, False).start()
        core_copy(1).start()

    def begin_z(r, mixed):
        for kind in range(2):
            z_copy(kind, r, mixed).start()

        @pl.when(r != LAST)
        def _():
            for kind in range(2, 4):
                z_copy(kind, r, mixed).start()

    def begin_x():
        for i in (2, 1, 3):
            x_send(i).start()
        mix[:, x] = own[LAST, :, x]

    def end_x():
        arrived(mix.at[:, pl.ds(0, 3)], x_r)
        begin_z(LAST, True)

    def stage_b(r, mixed):
        part = held(r, mixed)
        z_copy(0, r, mixed).wait_recv()
        part[lo, up] = part[lo, up] + b1p[r]
        z_copy(4, r, mixed).start()
        z_copy(1, r, mixed).wait_recv()
        part[hi, down] = part[hi, down] + b1m[r]
        z_copy(5, r, mixed).start()

        @pl.when(r == LAST)
        def _():
            for kind in range(2, 4):
                z_copy(kind, r, mixed).start()

    def stage_c(r, mixed):
        part = held(r, mixed)
        arrived(peer.at[r, lo], z_r.at[2, r])

        fin[pl.ds(0, HOMEB)] = (
            part[:, z].astype(F32) + b2p[r].astype(F32) + b2m[r].astype(F32)
        ).astype(BF)

        @pl.loop(0, N_FSDP)
        def _(o):
            snd[r, o] = fin[idx[1 if mixed else 0, o]]

        if mixed:
            @pl.loop(1, N_FSDP)
            def _(i):
                ex_send((h + 5 * i) % N_FSDP).start()

            @pl.when(y // 2 != core)
            def _():
                ex_send(h).start()

            @pl.when(y // 2 == core)
            def _():
                grad[y % 2, rows_of(2 * x + core, r)] = snd[r, h]
        else:
            rcv[r, h] = snd[r, h]

            @pl.loop(1, N_FSDP)
            def _(i):
                plane_send(r, (h + 5 * i) % N_FSDP).start()

    def stage_d(r):
        arrived(rcv.at[r, pl.ds(0, N_FSDP - 1)], pl_r.at[r])
        grad[:, rows_of(d, r)] = rcv[r, pl.ds(2 * d, 2)]

        @pl.loop(1, N_DP)
        def _(i):
            dp_send(r, (d + 3 * i) % N_DP).start()

    def roots_before(t):
        return jnp.clip(jnp.minimum(2 * (t - 2), t), 0, ROOT_STEPS)

    def either(t, *steps):
        return functools.reduce(jnp.logical_or, [t == step for step in steps])

    stage_a0()

    @pl.loop(1, STEPS)
    def _(t):
        @pl.when(t < R)
        def _():
            stage_a(jnp.where(t == 1, LAST, t - 1))

        @pl.when(either(t, 2, 3))
        def _():
            begin_z(t - 1, False)

        @pl.when(t == 1)
        def _():
            begin_x()

        @pl.when(t == 2)
        def _():
            begin()

        @pl.when(either(t, 2, 3, 4))
        def _():
            stage_b(t - 2, False)

        @pl.when(t == 5)
        def _():
            end_x()

        @pl.when(t == 6)
        def _():
            stage_b(LAST, True)

        @pl.when(either(t, 4, 5, 6))
        def _():
            stage_c(t - 4, False)

        @pl.when(either(t, 5, 6, 7))
        def _():
            stage_d(t - 5)

        @pl.when(t == 8)
        def _():
            stage_c(LAST, True)

        @pl.loop(roots_before(t), roots_before(t + 1))
        def _(step):
            root_step(step)

    arrived(rcv.at[pl.ds(0, LAST), pl.ds(0, 2 * N_DP - 2)], dp_r)

    @pl.when(y // 2 == core)
    def _():
        arrived(snd.at[LAST, pl.ds(0, N_FSDP - 1)], ex_r)

    @pl.when(y // 2 != core)
    def _():
        arrived(snd.at[LAST], ex_r)

    @pl.loop(0, 2)
    def _(j):
        g = grad[j]
        half = dot(keep[0, j], g).astype(BF)
        direction = dot(half, keep[1, j])
        g = g.astype(F32)
        count = float(BS * BS)
        grad_sq = jnp.sum(jnp.sum(g * g, axis=0, keepdims=True), axis=1, keepdims=True)
        dir_sq = jnp.sum(jnp.sum(direction * direction, axis=0, keepdims=True), axis=1, keepdims=True)
        ratio = jnp.sqrt(grad_sq / count) / jnp.sqrt(dir_sq / count + 1e-06)
        upd[j] = (-learn_rate * direction * ratio).astype(BF)
        for p in range(PIECES):
            turn[2 * d + j, p] = upd[j, piece(d, p)]

            @pl.loop(1, N_DP)
            def _(i):
                h1_send(j, p, (d + 3 * i) % N_DP).start()

    def forward(i, j, p):
        x = (d + 5 * i) % N_DP
        g = 2 * x + j

        @pl.when(i > 0)
        def _():
            arrived(turn.at[g, p], h1_r.at[g, p])

        @pl.when(g != h)
        def _():
            h2_send(g, p).start()

        @pl.when(g == h)
        def _():
            back[h, p] = turn[h, p]

    @pl.loop(0, 2)
    def _(j):
        @pl.loop(0, PIECES)
        def _(p):
            @pl.loop(0, N_DP)
            def _(i):
                forward(i, j, p)

    @pl.loop(0, 2)
    def _(j):
        g = grad[j]
        st[0, j] = decay_rate * st[0, j] + (1.0 - decay_rate) * dot(g, g, 1, 1)
        st[1, j] = decay_rate * st[1, j] + (1.0 - decay_rate) * dot(g, g, 0, 0)

    arrived(turn.at[pl.ds(0, N_FSDP - 1)], h2_r)

    left(own, 0)
    left(own.at[pl.ds(0, R - 1)], 1)
    left(mix.at[:, pl.ds(0, 3)], 2)
    left(snd.at[pl.ds(0, LAST), pl.ds(0, N_FSDP - 1)], 3)
    left(rcv.at[pl.ds(0, LAST), pl.ds(0, 2 * N_DP - 2)], 4)

    @pl.when(y // 2 == core)
    def _():
        left(snd.at[LAST, pl.ds(0, N_FSDP - 1)], 5)

    @pl.when(y // 2 != core)
    def _():
        left(snd.at[LAST], 5)

    left(upd.at[:, pl.ds(0, BS - ROWS)], 6)
    left(turn.at[pl.ds(0, N_FSDP - 1)], 7)


def finish(owner_in, back, st, keep, updates, out_sl, out_sr, out_rl, out_rr, owner, sem):
    h = lax.axis_index("fsdp")
    table = pltpu.make_async_copy(owner_in, owner, sem.at[8])
    table.start()
    copies = []
    for i in range(2):
        for j in range(2):
            copies.append(pltpu.make_async_copy(st.at[i, j], (out_sl, out_sr)[i].at[j], sem.at[2 * i + j]))
            copies.append(pltpu.make_async_copy(keep.at[i, j], (out_rl, out_rr)[i].at[j], sem.at[4 + 2 * i + j]))
    for copy in copies:
        copy.start()
    table.wait()
    for k in range(HOMEB):
        copies.append(pltpu.make_async_copy(back.at[owner[h * HOMEB + k]], updates.at[k], sem.at[9 + k]))
        copies[-1].start()
    for copy in copies:
        copy.wait()


def local(grads, owner, roster, left_stats, right_stats, left_root, right_root):
    anywhere = pl.BlockSpec(memory_space=pl.ANY)
    dma = pltpu.SemaphoreType.DMA
    shape = jax.ShapeDtypeStruct
    outs = pl.pallas_call(
        kernel,
        out_shape=(
            pltpu.VMEM((N_FSDP, PIECES, PIECE, BS), BF),
            pltpu.VMEM((2, 2, BS, BS), F32),
            pltpu.VMEM((2, 2, BS, BS), BF),
        ),
        in_specs=[anywhere] * 7,
        out_specs=[pl.BlockSpec(memory_space=pltpu.VMEM)] * 3,
        scratch_shapes=[
            pltpu.VMEM((R, HOMEB, NZ, RR, BS), BF),
            pltpu.VMEM((R, HOMEB, NZ, RR, BS), BF),
            pltpu.VMEM((HOMEB, NZ, RR, BS), BF),
            pltpu.VMEM((R, HALF, RR, BS), BF),
            pltpu.VMEM((R, HALF, RR, BS), BF),
            pltpu.VMEM((R, HOMEB, RR, BS), BF),
            pltpu.VMEM((R, HOMEB, RR, BS), BF),
            pltpu.VMEM((HOMEB + 1, RR, BS), BF),
            pltpu.VMEM((R, N_FSDP, RR, BS), BF),
            pltpu.VMEM((R, N_FSDP, RR, BS), BF),
            pltpu.VMEM((2, BS, BS), BF),
            pltpu.VMEM((2, BS, BS), BF),
            pltpu.VMEM((2, BS, BS), BF),
            pltpu.VMEM((2, BS, BS), BF),
            pltpu.VMEM((2, BS, BS), BF),
            pltpu.VMEM((N_FSDP, PIECES, PIECE, BS), BF),
            pltpu.SMEM((2, N_FSDP), jnp.int32),
            pltpu.SMEM((N_FSDP * HOMEB,), jnp.int32),
            pltpu.SMEM((N_FSDP * HOMEB,), jnp.int32),
            dma((R,)),
            dma((6,)),
            dma((8,)),
            dma((NZ,)),
            dma((R,)),
            dma,
            dma((3, R)),
            dma((LAST,)),
            dma,
            dma,
            dma((N_FSDP, PIECES)),
            dma,
        ],
        compiler_params=pltpu.CompilerParams(
            collective_id=0, has_side_effects=True, vmem_limit_bytes=40 * 1024 * 1024
        ),
        cost_estimate=pl.CostEstimate(flops=16 * 10**9, bytes_accessed=24 * 10**6, transcendentals=0),
        name="shampoo",
    )(
        *[
            pltpu.with_memory_space_constraint(array, pltpu.HBM)
            for array in (
                grads.reshape(HOMEB, NZ, 2, R, RR, BS), owner, roster,
                left_stats[0, 0], right_stats[0, 0], left_root[0, 0], right_root[0, 0],
            )
        ],
    )
    result, new_left, new_right, roots_left, roots_right = pl.pallas_call(
        finish,
        out_shape=(
            shape((HOMEB, PIECES, PIECE, BS), BF),
            shape((2, BS, BS), F32),
            shape((2, BS, BS), F32),
            shape((2, BS, BS), BF),
            shape((2, BS, BS), BF),
        ),
        in_specs=[anywhere] * 4,
        out_specs=[anywhere] * 5,
        scratch_shapes=[pltpu.SMEM((N_FSDP * HOMEB,), jnp.int32), dma((9 + HOMEB,))],
        compiler_params=pltpu.CompilerParams(vmem_limit_bytes=2 * 1024 * 1024),
        name="finish",
    )(
        pltpu.with_memory_space_constraint(owner, pltpu.HBM),
        *[pltpu.with_memory_space_constraint(out, pltpu.VMEM) for out in outs],
    )
    result = result.reshape(HOMEB, ROWS, BS)
    return (result, new_left[None, None], new_right[None, None], roots_left[None, None], roots_right[None, None])


def solution(mesh):
    placed = P("dp", "fsdp", None, None, None)
    return jax.shard_map(
        local,
        mesh=mesh,
        in_specs=(P("dp", "fsdp", None, None), P(), P(), placed, placed, placed, placed),
        out_specs=(P("fsdp", "dp", None), placed, placed, placed, placed),
        check_vma=False,
    )
```

```python
import functools

import jax
import jax.numpy as jnp
from jax import lax
from jax.experimental import pallas as pl
from jax.experimental.pallas import tpu as pltpu
from jax.sharding import PartitionSpec as P

BS = 512
HOMEB = 14
HALF = HOMEB // 2
NZ = 4
N_DP = 8
N_FSDP = 16
ROWS = BS // N_DP
R = 4
RR = ROWS // R
LAST = R - 1
ROOT_STEPS = 6
STEPS = 9
PIECES = 4
PIECE = ROWS // PIECES
decay_rate = 0.9
learn_rate = 10.0
BF = jnp.bfloat16
F32 = jnp.float32
MESH = pl.DeviceIdType.MESH


def dot(a, b, ca=1, cb=0):
    return lax.dot_general(a, b, (((ca,), (cb,)), ((), ())), preferred_element_type=F32)


def kernel(
    grads, owner_in, roster_in, left_stats, right_stats, left_root, right_root,
    back, st, keep,
    own, peer, mix, b1p, b1m, b2p, b2m, fin, snd, rcv, grad,
    mat, fac, cur, upd, turn, idx, owner, roster,
    own_sem, in_sem, sent, first_r, core_r, x_r, z_r, pl_r, dp_r, ex_r, h1_r, h2_r,
):
    d = lax.axis_index("dp")
    h = lax.axis_index("fsdp")
    z = d // 2
    core = d % 2
    x = h // 4
    y = h % 4
    up = (z + 1) % NZ
    down = (z + 3) % NZ
    far = (z + 2) % NZ

    def at_dp(x):
        return {"dp": x, "fsdp": h}

    def at_fsdp(x):
        return {"dp": d, "fsdp": x}

    def own_copy(r):
        return pltpu.make_async_copy(grads.at[:, :, core, r], own.at[r], own_sem.at[r])

    def remote(src, dst, s, r, dev):
        return pltpu.make_async_remote_copy(
            src_ref=src, dst_ref=dst, send_sem=s, recv_sem=r, device_id=dev, device_id_type=MESH
        )

    def core_copy(r):
        return remote(grads.at[:, :, 1 - core, r], peer.at[r], sent.at[0], core_r.at[r], at_dp(2 * z + 1 - core))

    def first_copy(i):
        q = (far, up, down, z)[i]
        return remote(
            grads.at[:, q, 1 - core, 0], peer.at[0, :, q], sent.at[0], first_r.at[i], at_dp(2 * z + 1 - core)
        )

    dev_up = at_dp(2 * up + core)
    dev_down = at_dp(2 * down + core)
    lo = pl.ds(0, HALF)
    hi = pl.ds(HALF, HALF)

    def held(r, mixed):
        return mix if mixed else own.at[r]

    def z_copy(kind, r, mixed):
        part = held(r, mixed)
        if kind == 0:
            src, dst, dev = part.at[lo, far], b1p.at[r], dev_up
        elif kind == 1:
            src, dst, dev = part.at[hi, far], b1m.at[r], dev_down
        elif kind == 2:
            src, dst, dev = part.at[hi, up], b2p.at[r, hi], dev_up
        elif kind == 3:
            src, dst, dev = part.at[lo, down], b2m.at[r, lo], dev_down
        elif kind == 4:
            src, dst, dev = part.at[lo, up], b2p.at[r, lo], dev_up
        else:
            src, dst, dev = part.at[hi, down], b2m.at[r, hi], dev_down
        return remote(src, dst, sent.at[1], z_r.at[min(kind, 2), r], dev)

    def x_send(i):
        q = (x + i) % 4
        return remote(own.at[LAST, :, q], mix.at[:, x], sent.at[2], x_r, at_fsdp(4 * q + y))

    def arrived(ref, semaphore):
        remote(ref, ref, sent.at[0], semaphore, dev_up).wait_recv()

    def left(ref, kind):
        remote(ref, ref, sent.at[kind], x_r, dev_up).wait_send()

    def plane_send(r, o):
        return remote(snd.at[r, o], rcv.at[r, h], sent.at[3], pl_r.at[r], at_fsdp(o))

    def rows_of(x, r):
        return pl.ds(pl.multiple_of(x * ROWS + r * RR, RR), RR)

    def dp_send(r, x):
        return remote(rcv.at[r, pl.ds(2 * x, 2)], grad.at[:, rows_of(d, r)], sent.at[4], dp_r, at_dp(x))

    def ex_send(o):
        return remote(
            snd.at[LAST, o], grad.at[y % 2, rows_of(2 * x + core, LAST)], sent.at[5], ex_r,
            {"dp": 2 * z + y // 2, "fsdp": o},
        )

    def chunk(x):
        return pl.ds(pl.multiple_of(x * ROWS, ROWS), ROWS)

    def piece(x, p):
        return pl.ds(pl.multiple_of(x * ROWS + p * PIECE, PIECE), PIECE)

    def h1_send(j, p, x):
        return remote(upd.at[j, piece(x, p)], turn.at[2 * d + j, p], sent.at[6], h1_r.at[2 * d + j, p], at_dp(x))

    def h2_send(g, p):
        return remote(turn.at[g, p], back.at[h, p], sent.at[7], h2_r, at_fsdp(g))

    def stat_in(i):
        return pltpu.make_async_copy((left_stats, right_stats)[i], st.at[i], in_sem.at[i])

    def keep_in(i):
        return pltpu.make_async_copy((left_root, right_root)[i], keep.at[i], in_sem.at[2 + i])

    tables = [
        pltpu.make_async_copy(owner_in, owner, in_sem.at[4]),
        pltpu.make_async_copy(roster_in, roster, in_sem.at[5]),
    ]
    for table in tables:
        table.start()

    @pl.loop(0, R)
    def _(r):
        own_copy(r).start()

    barrier = pltpu.get_barrier_semaphore()

    @pl.loop(0, N_DP)
    def _(i):
        there = {"dp": 2 * z + 1 - core, "fsdp": (i // 2) * 4 + 2 * core + i % 2}
        pl.semaphore_signal(barrier, inc=1, device_id=there, device_id_type=MESH)

    @pl.loop(1, N_FSDP)
    def _(i):
        pl.semaphore_signal(barrier, inc=1, device_id=at_fsdp((h + 5 * i) % N_FSDP), device_id_type=MESH)

    @pl.loop(1, N_DP)
    def _(i):
        pl.semaphore_signal(barrier, inc=1, device_id=at_dp((d + 3 * i) % N_DP), device_id_type=MESH)

    for i in range(2):
        stat_in(i).start()
    for i in range(2):
        keep_in(i).start()
    for table in tables:
        table.wait()

    @pl.loop(0, N_FSDP)
    def _(o):
        for i, home in enumerate((h, 4 * z + y)):
            place = jnp.int32(HOMEB)
            for k in range(HOMEB):
                place = jnp.where(owner[home * HOMEB + k] == o, jnp.int32(k), place)
            idx[i, o] = place

    fin[HOMEB] = jnp.zeros((RR, BS), BF)

    pl.semaphore_wait(barrier, N_DP + N_FSDP - 2 + jnp.where(y // 2 == core, 0, N_FSDP))

    for i in range(NZ):
        first_copy(i).start()
    core_copy(LAST).start()

    def begin():
        for i in range(2):
            stat_in(i).wait()
        for i in range(2):
            keep_in(i).wait()

    ii = lax.broadcasted_iota(jnp.int32, (BS, BS), 0)
    jj = lax.broadcasted_iota(jnp.int32, (BS, BS), 1)

    def factor(m):
        return (jnp.where(ii == jj, 1.25, 0.0) - 0.25 * m).astype(BF)

    def root_step(t):
        slot = t // 3
        sweep = t % 3

        @pl.when(sweep == 0)
        def _():
            for i in range(2):
                a = st[i, slot]
                bound = jnp.max(jnp.sum(jnp.abs(a), axis=0, keepdims=True), axis=1, keepdims=True)
                m = a * (1.0 / bound)
                f = factor(m)
                mat[i] = m.astype(BF)
                fac[i] = f
                first = lax.rsqrt(jnp.sqrt(bound)).astype(BF).astype(F32)
                cur[i] = (first * f.astype(F32)).astype(BF)

        for i in range(2):
            f = fac[i]
            f2 = dot(f, f).astype(BF)
            f4 = dot(f2, f2).astype(BF)
            m = dot(f4, mat[i])
            mat[i] = m.astype(BF)
            f = factor(m)
            fac[i] = f
            cur[i] = dot(cur[i], f).astype(BF)

        @pl.when(sweep == 2)
        def _():
            flag = jnp.int32(0)
            for k in range(HOMEB):
                spot = (2 * d + slot) * HOMEB + k
                flag += jnp.where(owner[spot] == h, roster[spot], 0)
            for i in range(2):
                keep[i, slot] = jnp.where(flag > 0, cur[i], keep[i, slot])

    def stage_a(r):
        own_copy(r).wait()
        core_copy(r).wait_recv()

        @pl.when(r == LAST)
        def _():
            core_copy(2).start()

        @pl.loop(0, HOMEB)
        def _(k):
            own[r, k] = own[r, k] + peer[r, k]

    def stage_a0():
        own_copy(0).wait()
        for i, q in enumerate((far, up, down, z)):
            first_copy(i).wait_recv()
            own[0, :, q] = own[0, :, q] + peer[0, :, q]
            for kind in ((0, 1), (2,), (3,), ())[i]:
                z_copy(kind, 0, False).start()
        core_copy(1).start()

    def begin_z(r, mixed):
        for kind in range(2):
            z_copy(kind, r, mixed).start()

        @pl.when(r != LAST)
        def _():
            for kind in range(2, 4):
                z_copy(kind, r, mixed).start()

    def begin_x():
        for i in (2, 1, 3):
            x_send(i).start()
        mix[:, x] = own[LAST, :, x]

    def end_x():
        arrived(mix.at[:, pl.ds(0, 3)], x_r)
        begin_z(LAST, True)

    def stage_b(r, mixed):
        part = held(r, mixed)
        z_copy(0, r, mixed).wait_recv()
        part[lo, up] = part[lo, up] + b1p[r]
        z_copy(4, r, mixed).start()
        z_copy(1, r, mixed).wait_recv()
        part[hi, down] = part[hi, down] + b1m[r]
        z_copy(5, r, mixed).start()

        @pl.when(r == LAST)
        def _():
            for kind in range(2, 4):
                z_copy(kind, r, mixed).start()

    def stage_c(r, mixed):
        part = held(r, mixed)
        arrived(peer.at[r, lo], z_r.at[2, r])

        fin[pl.ds(0, HOMEB)] = (
            part[:, z].astype(F32) + b2p[r].astype(F32) + b2m[r].astype(F32)
        ).astype(BF)

        @pl.loop(0, N_FSDP)
        def _(o):
            snd[r, o] = fin[idx[1 if mixed else 0, o]]

        if mixed:
            @pl.loop(1, N_FSDP)
            def _(i):
                ex_send((h + 5 * i) % N_FSDP).start()

            @pl.when(y // 2 != core)
            def _():
                ex_send(h).start()

            @pl.when(y // 2 == core)
            def _():
                grad[y % 2, rows_of(2 * x + core, r)] = snd[r, h]
        else:
            rcv[r, h] = snd[r, h]

            @pl.loop(1, N_FSDP)
            def _(i):
                plane_send(r, (h + 5 * i) % N_FSDP).start()

    def stage_d(r):
        arrived(rcv.at[r, pl.ds(0, N_FSDP - 1)], pl_r.at[r])
        grad[:, rows_of(d, r)] = rcv[r, pl.ds(2 * d, 2)]

        @pl.loop(1, N_DP)
        def _(i):
            dp_send(r, (d + 3 * i) % N_DP).start()

    def roots_before(t):
        return jnp.clip(jnp.minimum(2 * (t - 2), t), 0, ROOT_STEPS)

    def either(t, *steps):
        return functools.reduce(jnp.logical_or, [t == step for step in steps])

    stage_a0()

    @pl.loop(1, STEPS)
    def _(t):
        @pl.when(t < R)
        def _():
            stage_a(jnp.where(t == 1, LAST, t - 1))

        @pl.when(either(t, 2, 3))
        def _():
            begin_z(t - 1, False)

        @pl.when(t == 1)
        def _():
            begin_x()

        @pl.when(t == 2)
        def _():
            begin()

        @pl.when(either(t, 2, 3, 4))
        def _():
            stage_b(t - 2, False)

        @pl.when(either(t, 4, 5, 6))
        def _():
            stage_c(t - 4, False)

        @pl.when(t == 4)
        def _():
            end_x()

        @pl.when(t == 5)
        def _():
            stage_b(LAST, True)

        @pl.when(either(t, 5, 6, 7))
        def _():
            stage_d(t - 5)

        @pl.when(t == 8)
        def _():
            stage_c(LAST, True)

        @pl.loop(roots_before(t), roots_before(t + 1))
        def _(step):
            root_step(step)

    arrived(rcv.at[pl.ds(0, LAST), pl.ds(0, 2 * N_DP - 2)], dp_r)

    @pl.when(y // 2 == core)
    def _():
        arrived(snd.at[LAST, pl.ds(0, N_FSDP - 1)], ex_r)

    @pl.when(y // 2 != core)
    def _():
        arrived(snd.at[LAST], ex_r)

    @pl.loop(0, 2)
    def _(j):
        g = grad[j]
        half = dot(keep[0, j], g).astype(BF)
        direction = dot(half, keep[1, j])
        g = g.astype(F32)
        count = float(BS * BS)
        grad_sq = jnp.sum(jnp.sum(g * g, axis=0, keepdims=True), axis=1, keepdims=True)
        dir_sq = jnp.sum(jnp.sum(direction * direction, axis=0, keepdims=True), axis=1, keepdims=True)
        ratio = jnp.sqrt(grad_sq / count) / jnp.sqrt(dir_sq / count + 1e-06)
        upd[j] = (-learn_rate * direction * ratio).astype(BF)
        for p in range(PIECES):
            turn[2 * d + j, p] = upd[j, piece(d, p)]

    @pl.loop(0, PIECES)
    def _(p):
        @pl.loop(1, N_DP)
        def _(i):
            for j in range(2):
                h1_send(j, p, (d + 3 * i) % N_DP).start()

    def forward(i, j, p):
        x = (d + 5 * i) % N_DP
        g = 2 * x + j

        @pl.when(i > 0)
        def _():
            arrived(turn.at[g, p], h1_r.at[g, p])

        @pl.when(g != h)
        def _():
            h2_send(g, p).start()

        @pl.when(g == h)
        def _():
            back[h, p] = turn[h, p]

    @pl.loop(0, PIECES)
    def _(p):
        @pl.loop(0, N_DP)
        def _(i):
            for j in range(2):
                forward(i, j, p)

    @pl.loop(0, 2)
    def _(j):
        g = grad[j]
        st[0, j] = decay_rate * st[0, j] + (1.0 - decay_rate) * dot(g, g, 1, 1)
        st[1, j] = decay_rate * st[1, j] + (1.0 - decay_rate) * dot(g, g, 0, 0)

    arrived(turn.at[pl.ds(0, N_FSDP - 1)], h2_r)

    left(own, 0)
    left(own.at[pl.ds(0, R - 1)], 1)
    left(mix.at[:, pl.ds(0, 3)], 2)
    left(snd.at[pl.ds(0, LAST), pl.ds(0, N_FSDP - 1)], 3)
    left(rcv.at[pl.ds(0, LAST), pl.ds(0, 2 * N_DP - 2)], 4)

    @pl.when(y // 2 == core)
    def _():
        left(snd.at[LAST, pl.ds(0, N_FSDP - 1)], 5)

    @pl.when(y // 2 != core)
    def _():
        left(snd.at[LAST], 5)

    left(upd.at[:, pl.ds(0, BS - ROWS)], 6)
    left(turn.at[pl.ds(0, N_FSDP - 1)], 7)


def finish(owner_in, back, st, keep, updates, out_sl, out_sr, out_rl, out_rr, owner, sem):
    h = lax.axis_index("fsdp")
    table = pltpu.make_async_copy(owner_in, owner, sem.at[8])
    table.start()
    copies = []
    for i in range(2):
        for j in range(2):
            copies.append(pltpu.make_async_copy(st.at[i, j], (out_sl, out_sr)[i].at[j], sem.at[2 * i + j]))
            copies.append(pltpu.make_async_copy(keep.at[i, j], (out_rl, out_rr)[i].at[j], sem.at[4 + 2 * i + j]))
    for copy in copies:
        copy.start()
    table.wait()
    for k in range(HOMEB):
        copies.append(pltpu.make_async_copy(back.at[owner[h * HOMEB + k]], updates.at[k], sem.at[9 + k]))
        copies[-1].start()
    for copy in copies:
        copy.wait()


def local(grads, owner, roster, left_stats, right_stats, left_root, right_root):
    anywhere = pl.BlockSpec(memory_space=pl.ANY)
    dma = pltpu.SemaphoreType.DMA
    shape = jax.ShapeDtypeStruct
    outs = pl.pallas_call(
        kernel,
        out_shape=(
            pltpu.VMEM((N_FSDP, PIECES, PIECE, BS), BF),
            pltpu.VMEM((2, 2, BS, BS), F32),
            pltpu.VMEM((2, 2, BS, BS), BF),
        ),
        in_specs=[anywhere] * 7,
        out_specs=[pl.BlockSpec(memory_space=pltpu.VMEM)] * 3,
        scratch_shapes=[
            pltpu.VMEM((R, HOMEB, NZ, RR, BS), BF),
            pltpu.VMEM((R, HOMEB, NZ, RR, BS), BF),
            pltpu.VMEM((HOMEB, NZ, RR, BS), BF),
            pltpu.VMEM((R, HALF, RR, BS), BF),
            pltpu.VMEM((R, HALF, RR, BS), BF),
            pltpu.VMEM((R, HOMEB, RR, BS), BF),
            pltpu.VMEM((R, HOMEB, RR, BS), BF),
            pltpu.VMEM((HOMEB + 1, RR, BS), BF),
            pltpu.VMEM((R, N_FSDP, RR, BS), BF),
            pltpu.VMEM((R, N_FSDP, RR, BS), BF),
            pltpu.VMEM((2, BS, BS), BF),
            pltpu.VMEM((2, BS, BS), BF),
            pltpu.VMEM((2, BS, BS), BF),
            pltpu.VMEM((2, BS, BS), BF),
            pltpu.VMEM((2, BS, BS), BF),
            pltpu.VMEM((N_FSDP, PIECES, PIECE, BS), BF),
            pltpu.SMEM((2, N_FSDP), jnp.int32),
            pltpu.SMEM((N_FSDP * HOMEB,), jnp.int32),
            pltpu.SMEM((N_FSDP * HOMEB,), jnp.int32),
            dma((R,)),
            dma((6,)),
            dma((8,)),
            dma((NZ,)),
            dma((R,)),
            dma,
            dma((3, R)),
            dma((LAST,)),
            dma,
            dma,
            dma((N_FSDP, PIECES)),
            dma,
        ],
        compiler_params=pltpu.CompilerParams(
            collective_id=0, has_side_effects=True, vmem_limit_bytes=40 * 1024 * 1024
        ),
        cost_estimate=pl.CostEstimate(flops=16 * 10**9, bytes_accessed=24 * 10**6, transcendentals=0),
        name="shampoo",
    )(
        *[
            pltpu.with_memory_space_constraint(array, pltpu.HBM)
            for array in (
                grads.reshape(HOMEB, NZ, 2, R, RR, BS), owner, roster,
                left_stats[0, 0], right_stats[0, 0], left_root[0, 0], right_root[0, 0],
            )
        ],
    )
    result, new_left, new_right, roots_left, roots_right = pl.pallas_call(
        finish,
        out_shape=(
            shape((HOMEB, PIECES, PIECE, BS), BF),
            shape((2, BS, BS), F32),
            shape((2, BS, BS), F32),
            shape((2, BS, BS), BF),
            shape((2, BS, BS), BF),
        ),
        in_specs=[anywhere] * 4,
        out_specs=[anywhere] * 5,
        scratch_shapes=[pltpu.SMEM((N_FSDP * HOMEB,), jnp.int32), dma((9 + HOMEB,))],
        compiler_params=pltpu.CompilerParams(vmem_limit_bytes=2 * 1024 * 1024),
        name="finish",
    )(
        pltpu.with_memory_space_constraint(owner, pltpu.HBM),
        *[pltpu.with_memory_space_constraint(out, pltpu.VMEM) for out in outs],
    )
    result = result.reshape(HOMEB, ROWS, BS)
    return (result, new_left[None, None], new_right[None, None], roots_left[None, None], roots_right[None, None])


def solution(mesh):
    placed = P("dp", "fsdp", None, None, None)
    return jax.shard_map(
        local,
        mesh=mesh,
        in_specs=(P("dp", "fsdp", None, None), P(), P(), placed, placed, placed, placed),
        out_specs=(P("fsdp", "dp", None), placed, placed, placed, placed),
        check_vma=False,
    )
```

```python
import functools

import jax
import jax.numpy as jnp
from jax import lax
from jax.experimental import pallas as pl
from jax.experimental.pallas import tpu as pltpu
from jax.sharding import PartitionSpec as P

BS = 512
HOMEB = 14
HALF = HOMEB // 2
NZ = 4
N_DP = 8
N_FSDP = 16
ROWS = BS // N_DP
R = 4
RR = ROWS // R
LAST = R - 1
ROOT_STEPS = 6
STEPS = 9
PIECES = 4
PIECE = ROWS // PIECES
decay_rate = 0.9
learn_rate = 10.0
BF = jnp.bfloat16
F32 = jnp.float32
MESH = pl.DeviceIdType.MESH


def dot(a, b, ca=1, cb=0):
    return lax.dot_general(a, b, (((ca,), (cb,)), ((), ())), preferred_element_type=F32)


def kernel(
    grads, owner_in, roster_in, left_stats, right_stats, left_root, right_root,
    back, st, keep,
    own, peer, mix, b1p, b1m, b2p, b2m, fin, snd, rcv, grad,
    mat, fac, cur, upd, turn, idx, owner, roster,
    own_sem, in_sem, sent, first_r, core_r, x_r, z_r, pl_r, dp_r, ex_r, h1_r, h2_r,
):
    d = lax.axis_index("dp")
    h = lax.axis_index("fsdp")
    z = d // 2
    core = d % 2
    x = h // 4
    y = h % 4
    up = (z + 1) % NZ
    down = (z + 3) % NZ
    far = (z + 2) % NZ

    def at_dp(x):
        return {"dp": x, "fsdp": h}

    def at_fsdp(x):
        return {"dp": d, "fsdp": x}

    def own_copy(r):
        return pltpu.make_async_copy(grads.at[:, :, core, r], own.at[r], own_sem.at[r])

    def remote(src, dst, s, r, dev):
        return pltpu.make_async_remote_copy(
            src_ref=src, dst_ref=dst, send_sem=s, recv_sem=r, device_id=dev, device_id_type=MESH
        )

    def core_copy(r):
        return remote(grads.at[:, :, 1 - core, r], peer.at[r], sent.at[0], core_r.at[r], at_dp(2 * z + 1 - core))

    def first_copy(i):
        q = (far, up, down, z)[i]
        return remote(
            grads.at[:, q, 1 - core, 0], peer.at[0, :, q], sent.at[0], first_r.at[i], at_dp(2 * z + 1 - core)
        )

    dev_up = at_dp(2 * up + core)
    dev_down = at_dp(2 * down + core)
    lo = pl.ds(0, HALF)
    hi = pl.ds(HALF, HALF)

    def held(r, mixed):
        return mix if mixed else own.at[r]

    def z_copy(kind, r, mixed):
        part = held(r, mixed)
        if kind == 0:
            src, dst, dev = part.at[lo, far], b1p.at[r], dev_up
        elif kind == 1:
            src, dst, dev = part.at[hi, far], b1m.at[r], dev_down
        elif kind == 2:
            src, dst, dev = part.at[hi, up], b2p.at[r, hi], dev_up
        elif kind == 3:
            src, dst, dev = part.at[lo, down], b2m.at[r, lo], dev_down
        elif kind == 4:
            src, dst, dev = part.at[lo, up], b2p.at[r, lo], dev_up
        else:
            src, dst, dev = part.at[hi, down], b2m.at[r, hi], dev_down
        return remote(src, dst, sent.at[1], z_r.at[min(kind, 2), r], dev)

    def x_send(i):
        q = (x + i) % 4
        return remote(own.at[LAST, :, q], mix.at[:, x], sent.at[2], x_r, at_fsdp(4 * q + y))

    def arrived(ref, semaphore):
        remote(ref, ref, sent.at[0], semaphore, dev_up).wait_recv()

    def left(ref, kind):
        remote(ref, ref, sent.at[kind], x_r, dev_up).wait_send()

    def plane_send(r, o):
        return remote(snd.at[r, o], rcv.at[r, h], sent.at[3], pl_r.at[r], at_fsdp(o))

    def rows_of(x, r):
        return pl.ds(pl.multiple_of(x * ROWS + r * RR, RR), RR)

    def dp_send(r, x):
        return remote(rcv.at[r, pl.ds(2 * x, 2)], grad.at[:, rows_of(d, r)], sent.at[4], dp_r, at_dp(x))

    def ex_send(o):
        return remote(
            snd.at[LAST, o], grad.at[y % 2, rows_of(2 * x + core, LAST)], sent.at[5], ex_r,
            {"dp": 2 * z + y // 2, "fsdp": o},
        )

    def chunk(x):
        return pl.ds(pl.multiple_of(x * ROWS, ROWS), ROWS)

    def piece(x, p):
        return pl.ds(pl.multiple_of(x * ROWS + p * PIECE, PIECE), PIECE)

    def h1_send(j, p, x):
        return remote(upd.at[j, piece(x, p)], turn.at[2 * d + j, p], sent.at[6], h1_r.at[2 * d + j, p], at_dp(x))

    def h2_send(g, p):
        return remote(turn.at[g, p], back.at[h, p], sent.at[7], h2_r, at_fsdp(g))

    def stat_in(i):
        return pltpu.make_async_copy((left_stats, right_stats)[i], st.at[i], in_sem.at[i])

    def keep_in(i):
        return pltpu.make_async_copy((left_root, right_root)[i], keep.at[i], in_sem.at[2 + i])

    tables = [
        pltpu.make_async_copy(owner_in, owner, in_sem.at[4]),
        pltpu.make_async_copy(roster_in, roster, in_sem.at[5]),
    ]
    for table in tables:
        table.start()

    @pl.loop(0, R)
    def _(r):
        own_copy(r).start()

    barrier = pltpu.get_barrier_semaphore()

    @pl.loop(0, N_DP)
    def _(i):
        there = {"dp": 2 * z + 1 - core, "fsdp": (i // 2) * 4 + 2 * core + i % 2}
        pl.semaphore_signal(barrier, inc=1, device_id=there, device_id_type=MESH)

    @pl.loop(1, N_FSDP)
    def _(i):
        pl.semaphore_signal(barrier, inc=1, device_id=at_fsdp((h + 5 * i) % N_FSDP), device_id_type=MESH)

    @pl.loop(1, N_DP)
    def _(i):
        pl.semaphore_signal(barrier, inc=1, device_id=at_dp((d + 3 * i) % N_DP), device_id_type=MESH)

    for i in range(2):
        stat_in(i).start()
    for i in range(2):
        keep_in(i).start()
    for table in tables:
        table.wait()

    @pl.loop(0, N_FSDP)
    def _(o):
        for i, home in enumerate((h, 4 * z + y)):
            place = jnp.int32(HOMEB)
            for k in range(HOMEB):
                place = jnp.where(owner[home * HOMEB + k] == o, jnp.int32(k), place)
            idx[i, o] = place

    fin[HOMEB] = jnp.zeros((RR, BS), BF)

    pl.semaphore_wait(barrier, N_DP + N_FSDP - 2 + jnp.where(y // 2 == core, 0, N_FSDP))

    for i in range(NZ):
        first_copy(i).start()
    core_copy(LAST).start()

    def begin():
        for i in range(2):
            stat_in(i).wait()
        for i in range(2):
            keep_in(i).wait()

    ii = lax.broadcasted_iota(jnp.int32, (BS, BS), 0)
    jj = lax.broadcasted_iota(jnp.int32, (BS, BS), 1)

    def factor(m):
        return (jnp.where(ii == jj, 1.25, 0.0) - 0.25 * m).astype(BF)

    def root_step(t):
        slot = t // 3
        sweep = t % 3

        @pl.when(sweep == 0)
        def _():
            for i in range(2):
                a = st[i, slot]
                bound = jnp.max(jnp.sum(jnp.abs(a), axis=0, keepdims=True), axis=1, keepdims=True)
                m = a * (1.0 / bound)
                f = factor(m)
                mat[i] = m.astype(BF)
                fac[i] = f
                first = lax.rsqrt(jnp.sqrt(bound)).astype(BF).astype(F32)
                cur[i] = (first * f.astype(F32)).astype(BF)

        for i in range(2):
            f = fac[i]
            f2 = dot(f, f).astype(BF)
            f4 = dot(f2, f2).astype(BF)
            m = dot(f4, mat[i])
            mat[i] = m.astype(BF)
            f = factor(m)
            fac[i] = f
            cur[i] = dot(cur[i], f).astype(BF)

        @pl.when(sweep == 2)
        def _():
            flag = jnp.int32(0)
            for k in range(HOMEB):
                spot = (2 * d + slot) * HOMEB + k
                flag += jnp.where(owner[spot] == h, roster[spot], 0)
            for i in range(2):
                keep[i, slot] = jnp.where(flag > 0, cur[i], keep[i, slot])

    def stage_a(r):
        own_copy(r).wait()
        core_copy(r).wait_recv()

        @pl.when(r == LAST)
        def _():
            core_copy(2).start()

        @pl.loop(0, HOMEB)
        def _(k):
            own[r, k] = own[r, k] + peer[r, k]

    def stage_a0():
        own_copy(0).wait()
        for i, q in enumerate((far, up, down, z)):
            first_copy(i).wait_recv()
            own[0, :, q] = own[0, :, q] + peer[0, :, q]
            for kind in ((0, 1), (2,), (3,), ())[i]:
                z_copy(kind, 0, False).start()
        core_copy(1).start()

    def begin_z(r, mixed):
        for kind in range(2):
            z_copy(kind, r, mixed).start()

        @pl.when(r < 2)
        def _():
            for kind in range(2, 4):
                z_copy(kind, r, mixed).start()

    def begin_x():
        for i in (2, 1, 3):
            x_send(i).start()
        mix[:, x] = own[LAST, :, x]

    def end_x():
        arrived(mix.at[:, pl.ds(0, 3)], x_r)
        begin_z(LAST, True)
        for kind in range(2, 4):
            z_copy(kind, 2, False).start()
            z_copy(kind, LAST, True).start()

    def stage_b(r, mixed):
        part = held(r, mixed)
        z_copy(0, r, mixed).wait_recv()
        part[lo, up] = part[lo, up] + b1p[r]
        z_copy(4, r, mixed).start()
        z_copy(1, r, mixed).wait_recv()
        part[hi, down] = part[hi, down] + b1m[r]
        z_copy(5, r, mixed).start()

    def stage_c(r, mixed):
        part = held(r, mixed)
        arrived(peer.at[r, lo], z_r.at[2, r])

        fin[pl.ds(0, HOMEB)] = (
            part[:, z].astype(F32) + b2p[r].astype(F32) + b2m[r].astype(F32)
        ).astype(BF)

        @pl.loop(0, N_FSDP)
        def _(o):
            snd[r, o] = fin[idx[1 if mixed else 0, o]]

        if mixed:
            @pl.loop(1, N_FSDP)
            def _(i):
                ex_send((h + 5 * i) % N_FSDP).start()

            @pl.when(y // 2 != core)
            def _():
                ex_send(h).start()

            @pl.when(y // 2 == core)
            def _():
                grad[y % 2, rows_of(2 * x + core, r)] = snd[r, h]
        else:
            rcv[r, h] = snd[r, h]

            @pl.loop(1, N_FSDP)
            def _(i):
                plane_send(r, (h + 5 * i) % N_FSDP).start()

    def stage_d(r):
        arrived(rcv.at[r, pl.ds(0, N_FSDP - 1)], pl_r.at[r])
        grad[:, rows_of(d, r)] = rcv[r, pl.ds(2 * d, 2)]

        @pl.loop(1, N_DP)
        def _(i):
            dp_send(r, (d + 3 * i) % N_DP).start()

    def roots_before(t):
        return jnp.clip(jnp.where(t < 4, 2 * (t - 2), 2 * t - 5), 0, ROOT_STEPS)

    def either(t, *steps):
        return functools.reduce(jnp.logical_or, [t == step for step in steps])

    stage_a0()

    @pl.loop(1, STEPS)
    def _(t):
        @pl.when(t < R)
        def _():
            stage_a(jnp.where(t == 1, LAST, t - 1))

        @pl.when(either(t, 2, 3))
        def _():
            begin_z(t - 1, False)

        @pl.when(t == 1)
        def _():
            begin_x()

        @pl.when(t == 2)
        def _():
            begin()

        @pl.when(either(t, 2, 3, 4))
        def _():
            stage_b(t - 2, False)

        @pl.when(either(t, 4, 5, 6))
        def _():
            stage_c(t - 4, False)

        @pl.when(t == 4)
        def _():
            end_x()

        @pl.when(t == 5)
        def _():
            stage_b(LAST, True)

        @pl.when(either(t, 5, 6, 7))
        def _():
            stage_d(t - 5)

        @pl.when(t == 8)
        def _():
            stage_c(LAST, True)

        @pl.loop(roots_before(t), roots_before(t + 1))
        def _(step):
            root_step(step)

    arrived(rcv.at[pl.ds(0, LAST), pl.ds(0, 2 * N_DP - 2)], dp_r)

    @pl.when(y // 2 == core)
    def _():
        arrived(snd.at[LAST, pl.ds(0, N_FSDP - 1)], ex_r)

    @pl.when(y // 2 != core)
    def _():
        arrived(snd.at[LAST], ex_r)

    @pl.loop(0, 2)
    def _(j):
        g = grad[j]
        half = dot(keep[0, j], g).astype(BF)
        direction = dot(half, keep[1, j])
        g = g.astype(F32)
        count = float(BS * BS)
        grad_sq = jnp.sum(jnp.sum(g * g, axis=0, keepdims=True), axis=1, keepdims=True)
        dir_sq = jnp.sum(jnp.sum(direction * direction, axis=0, keepdims=True), axis=1, keepdims=True)
        ratio = jnp.sqrt(grad_sq / count) / jnp.sqrt(dir_sq / count + 1e-06)
        upd[j] = (-learn_rate * direction * ratio).astype(BF)
        for p in range(PIECES):
            turn[2 * d + j, p] = upd[j, piece(d, p)]

    @pl.loop(0, PIECES)
    def _(p):
        @pl.loop(1, N_DP)
        def _(i):
            for j in range(2):
                h1_send(j, p, (d + 3 * i) % N_DP).start()

    def forward(i, j, p):
        x = (d + 5 * i) % N_DP
        g = 2 * x + j

        @pl.when(i > 0)
        def _():
            arrived(turn.at[g, p], h1_r.at[g, p])

        @pl.when(g != h)
        def _():
            h2_send(g, p).start()

        @pl.when(g == h)
        def _():
            back[h, p] = turn[h, p]

    @pl.loop(0, PIECES)
    def _(p):
        @pl.loop(0, N_DP)
        def _(i):
            for j in range(2):
                forward(i, j, p)

    @pl.loop(0, 2)
    def _(j):
        g = grad[j]
        st[0, j] = decay_rate * st[0, j] + (1.0 - decay_rate) * dot(g, g, 1, 1)
        st[1, j] = decay_rate * st[1, j] + (1.0 - decay_rate) * dot(g, g, 0, 0)

    arrived(turn.at[pl.ds(0, N_FSDP - 1)], h2_r)

    left(own, 0)
    left(own.at[pl.ds(0, R - 1)], 1)
    left(mix.at[:, pl.ds(0, 3)], 2)
    left(snd.at[pl.ds(0, LAST), pl.ds(0, N_FSDP - 1)], 3)
    left(rcv.at[pl.ds(0, LAST), pl.ds(0, 2 * N_DP - 2)], 4)

    @pl.when(y // 2 == core)
    def _():
        left(snd.at[LAST, pl.ds(0, N_FSDP - 1)], 5)

    @pl.when(y // 2 != core)
    def _():
        left(snd.at[LAST], 5)

    left(upd.at[:, pl.ds(0, BS - ROWS)], 6)
    left(turn.at[pl.ds(0, N_FSDP - 1)], 7)


def finish(owner_in, back, st, keep, updates, out_sl, out_sr, out_rl, out_rr, owner, sem):
    h = lax.axis_index("fsdp")
    table = pltpu.make_async_copy(owner_in, owner, sem.at[8])
    table.start()
    copies = []
    for i in range(2):
        for j in range(2):
            copies.append(pltpu.make_async_copy(st.at[i, j], (out_sl, out_sr)[i].at[j], sem.at[2 * i + j]))
            copies.append(pltpu.make_async_copy(keep.at[i, j], (out_rl, out_rr)[i].at[j], sem.at[4 + 2 * i + j]))
    for copy in copies:
        copy.start()
    table.wait()
    for k in range(HOMEB):
        copies.append(pltpu.make_async_copy(back.at[owner[h * HOMEB + k]], updates.at[k], sem.at[9 + k]))
        copies[-1].start()
    for copy in copies:
        copy.wait()


def local(grads, owner, roster, left_stats, right_stats, left_root, right_root):
    anywhere = pl.BlockSpec(memory_space=pl.ANY)
    dma = pltpu.SemaphoreType.DMA
    shape = jax.ShapeDtypeStruct
    outs = pl.pallas_call(
        kernel,
        out_shape=(
            pltpu.VMEM((N_FSDP, PIECES, PIECE, BS), BF),
            pltpu.VMEM((2, 2, BS, BS), F32),
            pltpu.VMEM((2, 2, BS, BS), BF),
        ),
        in_specs=[anywhere] * 7,
        out_specs=[pl.BlockSpec(memory_space=pltpu.VMEM)] * 3,
        scratch_shapes=[
            pltpu.VMEM((R, HOMEB, NZ, RR, BS), BF),
            pltpu.VMEM((R, HOMEB, NZ, RR, BS), BF),
            pltpu.VMEM((HOMEB, NZ, RR, BS), BF),
            pltpu.VMEM((R, HALF, RR, BS), BF),
            pltpu.VMEM((R, HALF, RR, BS), BF),
            pltpu.VMEM((R, HOMEB, RR, BS), BF),
            pltpu.VMEM((R, HOMEB, RR, BS), BF),
            pltpu.VMEM((HOMEB + 1, RR, BS), BF),
            pltpu.VMEM((R, N_FSDP, RR, BS), BF),
            pltpu.VMEM((R, N_FSDP, RR, BS), BF),
            pltpu.VMEM((2, BS, BS), BF),
            pltpu.VMEM((2, BS, BS), BF),
            pltpu.VMEM((2, BS, BS), BF),
            pltpu.VMEM((2, BS, BS), BF),
            pltpu.VMEM((2, BS, BS), BF),
            pltpu.VMEM((N_FSDP, PIECES, PIECE, BS), BF),
            pltpu.SMEM((2, N_FSDP), jnp.int32),
            pltpu.SMEM((N_FSDP * HOMEB,), jnp.int32),
            pltpu.SMEM((N_FSDP * HOMEB,), jnp.int32),
            dma((R,)),
            dma((6,)),
            dma((8,)),
            dma((NZ,)),
            dma((R,)),
            dma,
            dma((3, R)),
            dma((LAST,)),
            dma,
            dma,
            dma((N_FSDP, PIECES)),
            dma,
        ],
        compiler_params=pltpu.CompilerParams(
            collective_id=0, has_side_effects=True, vmem_limit_bytes=40 * 1024 * 1024
        ),
        cost_estimate=pl.CostEstimate(flops=16 * 10**9, bytes_accessed=24 * 10**6, transcendentals=0),
        name="shampoo",
    )(
        *[
            pltpu.with_memory_space_constraint(array, pltpu.HBM)
            for array in (
                grads.reshape(HOMEB, NZ, 2, R, RR, BS), owner, roster,
                left_stats[0, 0], right_stats[0, 0], left_root[0, 0], right_root[0, 0],
            )
        ],
    )
    result, new_left, new_right, roots_left, roots_right = pl.pallas_call(
        finish,
        out_shape=(
            shape((HOMEB, PIECES, PIECE, BS), BF),
            shape((2, BS, BS), F32),
            shape((2, BS, BS), F32),
            shape((2, BS, BS), BF),
            shape((2, BS, BS), BF),
        ),
        in_specs=[anywhere] * 4,
        out_specs=[anywhere] * 5,
        scratch_shapes=[pltpu.SMEM((N_FSDP * HOMEB,), jnp.int32), dma((9 + HOMEB,))],
        compiler_params=pltpu.CompilerParams(vmem_limit_bytes=2 * 1024 * 1024),
        name="finish",
    )(
        pltpu.with_memory_space_constraint(owner, pltpu.HBM),
        *[pltpu.with_memory_space_constraint(out, pltpu.VMEM) for out in outs],
    )
    result = result.reshape(HOMEB, ROWS, BS)
    return (result, new_left[None, None], new_right[None, None], roots_left[None, None], roots_right[None, None])


def solution(mesh):
    placed = P("dp", "fsdp", None, None, None)
    return jax.shard_map(
        local,
        mesh=mesh,
        in_specs=(P("dp", "fsdp", None, None), P(), P(), placed, placed, placed, placed),
        out_specs=(P("fsdp", "dp", None), placed, placed, placed, placed),
        check_vma=False,
    )
```

```python
import functools

import jax
import jax.numpy as jnp
from jax import lax
from jax.experimental import pallas as pl
from jax.experimental.pallas import tpu as pltpu
from jax.sharding import PartitionSpec as P

BS = 512
HOMEB = 14
HALF = HOMEB // 2
NZ = 4
N_DP = 8
N_FSDP = 16
ROWS = BS // N_DP
R = 4
RR = ROWS // R
LAST = R - 1
ROOT_STEPS = 6
STEPS = 8
PIECES = 4
PIECE = ROWS // PIECES
decay_rate = 0.9
learn_rate = 10.0
BF = jnp.bfloat16
F32 = jnp.float32
MESH = pl.DeviceIdType.MESH


def dot(a, b, ca=1, cb=0):
    return lax.dot_general(a, b, (((ca,), (cb,)), ((), ())), preferred_element_type=F32)


def kernel(
    grads, owner_in, roster_in, left_stats, right_stats, left_root, right_root,
    back, st, keep,
    own, peer, mix, b1p, b1m, b2p, b2m, fin, snd, rcv, grad,
    mat, fac, cur, upd, turn, idx, owner, roster,
    own_sem, in_sem, sent, first_r, core_r, x_r, z_r, pl_r, dp_r, ex_r, h1_r, h2_r,
):
    d = lax.axis_index("dp")
    h = lax.axis_index("fsdp")
    z = d // 2
    core = d % 2
    x = h // 4
    y = h % 4
    up = (z + 1) % NZ
    down = (z + 3) % NZ
    far = (z + 2) % NZ

    def at_dp(x):
        return {"dp": x, "fsdp": h}

    def at_fsdp(x):
        return {"dp": d, "fsdp": x}

    def own_copy(r):
        return pltpu.make_async_copy(grads.at[:, :, core, r], own.at[r], own_sem.at[r])

    def remote(src, dst, s, r, dev):
        return pltpu.make_async_remote_copy(
            src_ref=src, dst_ref=dst, send_sem=s, recv_sem=r, device_id=dev, device_id_type=MESH
        )

    def core_copy(r):
        return remote(grads.at[:, :, 1 - core, r], peer.at[r], sent.at[0], core_r.at[r], at_dp(2 * z + 1 - core))

    def first_copy(i):
        q = (far, up, down, z)[i]
        return remote(
            grads.at[:, q, 1 - core, 0], peer.at[0, :, q], sent.at[0], first_r.at[i], at_dp(2 * z + 1 - core)
        )

    dev_up = at_dp(2 * up + core)
    dev_down = at_dp(2 * down + core)
    lo = pl.ds(0, HALF)
    hi = pl.ds(HALF, HALF)

    def held(r, mixed):
        return mix if mixed else own.at[r]

    def z_copy(kind, r, mixed):
        part = held(r, mixed)
        if kind == 0:
            src, dst, dev = part.at[lo, far], b1p.at[r], dev_up
        elif kind == 1:
            src, dst, dev = part.at[hi, far], b1m.at[r], dev_down
        elif kind == 2:
            src, dst, dev = part.at[hi, up], b2p.at[r, hi], dev_up
        elif kind == 3:
            src, dst, dev = part.at[lo, down], b2m.at[r, lo], dev_down
        elif kind == 4:
            src, dst, dev = part.at[lo, up], b2p.at[r, lo], dev_up
        else:
            src, dst, dev = part.at[hi, down], b2m.at[r, hi], dev_down
        return remote(src, dst, sent.at[1], z_r.at[min(kind, 2), r], dev)

    def x_send(i):
        q = (x + i) % 4
        return remote(own.at[LAST, :, q], mix.at[:, x], sent.at[2], x_r, at_fsdp(4 * q + y))

    def arrived(ref, semaphore):
        remote(ref, ref, sent.at[0], semaphore, dev_up).wait_recv()

    def left(ref, kind):
        remote(ref, ref, sent.at[kind], x_r, dev_up).wait_send()

    def plane_send(r, o):
        return remote(snd.at[r, o], rcv.at[r, h], sent.at[3], pl_r.at[r], at_fsdp(o))

    def rows_of(x, r):
        return pl.ds(pl.multiple_of(x * ROWS + r * RR, RR), RR)

    def dp_send(r, x):
        return remote(rcv.at[r, pl.ds(2 * x, 2)], grad.at[:, rows_of(d, r)], sent.at[4], dp_r, at_dp(x))

    def ex_send(o):
        return remote(
            snd.at[LAST, o], grad.at[y % 2, rows_of(2 * x + core, LAST)], sent.at[5], ex_r,
            {"dp": 2 * z + y // 2, "fsdp": o},
        )

    def chunk(x):
        return pl.ds(pl.multiple_of(x * ROWS, ROWS), ROWS)

    def piece(x, p):
        return pl.ds(pl.multiple_of(x * ROWS + p * PIECE, PIECE), PIECE)

    def h1_send(j, p, x):
        return remote(upd.at[j, piece(x, p)], turn.at[2 * d + j, p], sent.at[6], h1_r.at[2 * d + j, p], at_dp(x))

    def h2_send(g, p):
        return remote(turn.at[g, p], back.at[h, p], sent.at[7], h2_r, at_fsdp(g))

    def stat_in(i):
        return pltpu.make_async_copy((left_stats, right_stats)[i], st.at[i], in_sem.at[i])

    def keep_in(i):
        return pltpu.make_async_copy((left_root, right_root)[i], keep.at[i], in_sem.at[2 + i])

    tables = [
        pltpu.make_async_copy(owner_in, owner, in_sem.at[4]),
        pltpu.make_async_copy(roster_in, roster, in_sem.at[5]),
    ]
    for table in tables:
        table.start()

    @pl.loop(0, R)
    def _(r):
        own_copy(r).start()

    barrier = pltpu.get_barrier_semaphore()

    @pl.loop(0, N_DP)
    def _(i):
        there = {"dp": 2 * z + 1 - core, "fsdp": (i // 2) * 4 + 2 * core + i % 2}
        pl.semaphore_signal(barrier, inc=1, device_id=there, device_id_type=MESH)

    @pl.loop(1, N_FSDP)
    def _(i):
        pl.semaphore_signal(barrier, inc=1, device_id=at_fsdp((h + 5 * i) % N_FSDP), device_id_type=MESH)

    @pl.loop(1, N_DP)
    def _(i):
        pl.semaphore_signal(barrier, inc=1, device_id=at_dp((d + 3 * i) % N_DP), device_id_type=MESH)

    for i in range(2):
        stat_in(i).start()
    for i in range(2):
        keep_in(i).start()
    for table in tables:
        table.wait()

    @pl.loop(0, N_FSDP)
    def _(o):
        for i, home in enumerate((h, 4 * z + y)):
            place = jnp.int32(HOMEB)
            for k in range(HOMEB):
                place = jnp.where(owner[home * HOMEB + k] == o, jnp.int32(k), place)
            idx[i, o] = place

    fin[HOMEB] = jnp.zeros((RR, BS), BF)

    pl.semaphore_wait(barrier, N_DP + N_FSDP - 2 + jnp.where(y // 2 == core, 0, N_FSDP))

    for i in range(NZ):
        first_copy(i).start()
    core_copy(LAST).start()

    def begin():
        for i in range(2):
            stat_in(i).wait()
        for i in range(2):
            keep_in(i).wait()

    ii = lax.broadcasted_iota(jnp.int32, (BS, BS), 0)
    jj = lax.broadcasted_iota(jnp.int32, (BS, BS), 1)

    def factor(m):
        return (jnp.where(ii == jj, 1.25, 0.0) - 0.25 * m).astype(BF)

    def root_step(t):
        slot = t // 3
        sweep = t % 3

        @pl.when(sweep == 0)
        def _():
            for i in range(2):
                a = st[i, slot]
                bound = jnp.max(jnp.sum(jnp.abs(a), axis=0, keepdims=True), axis=1, keepdims=True)
                m = a * (1.0 / bound)
                f = factor(m)
                mat[i] = m.astype(BF)
                fac[i] = f
                first = lax.rsqrt(jnp.sqrt(bound)).astype(BF).astype(F32)
                cur[i] = (first * f.astype(F32)).astype(BF)

        for i in range(2):
            f = fac[i]
            f2 = dot(f, f).astype(BF)
            f4 = dot(f2, f2).astype(BF)
            m = dot(f4, mat[i])
            mat[i] = m.astype(BF)
            f = factor(m)
            fac[i] = f
            cur[i] = dot(cur[i], f).astype(BF)

        @pl.when(sweep == 2)
        def _():
            flag = jnp.int32(0)
            for k in range(HOMEB):
                spot = (2 * d + slot) * HOMEB + k
                flag += jnp.where(owner[spot] == h, roster[spot], 0)
            for i in range(2):
                keep[i, slot] = jnp.where(flag > 0, cur[i], keep[i, slot])

    def stage_a(r):
        own_copy(r).wait()
        core_copy(r).wait_recv()

        @pl.when(r == LAST)
        def _():
            core_copy(2).start()

        @pl.loop(0, HOMEB)
        def _(k):
            own[r, k] = own[r, k] + peer[r, k]

    def stage_a0():
        own_copy(0).wait()
        for i, q in enumerate((far, up, down, z)):
            first_copy(i).wait_recv()
            own[0, :, q] = own[0, :, q] + peer[0, :, q]
            for kind in ((0, 1), (2,), (3,), ())[i]:
                z_copy(kind, 0, False).start()
        core_copy(1).start()

    def begin_z(r, mixed):
        for kind in range(2):
            z_copy(kind, r, mixed).start()

        @pl.when(r < 2)
        def _():
            for kind in range(2, 4):
                z_copy(kind, r, mixed).start()

    def begin_x():
        for i in (2, 1, 3):
            x_send(i).start()
        mix[:, x] = own[LAST, :, x]

    def end_x():
        arrived(mix.at[:, pl.ds(0, 3)], x_r)
        begin_z(LAST, True)
        for kind in range(2, 4):
            z_copy(kind, 2, False).start()
            z_copy(kind, LAST, True).start()

    def stage_b(r, mixed):
        part = held(r, mixed)
        z_copy(0, r, mixed).wait_recv()
        part[lo, up] = part[lo, up] + b1p[r]
        z_copy(4, r, mixed).start()
        z_copy(1, r, mixed).wait_recv()
        part[hi, down] = part[hi, down] + b1m[r]
        z_copy(5, r, mixed).start()

    def stage_c(r, mixed):
        part = held(r, mixed)
        arrived(peer.at[r, lo], z_r.at[2, r])

        fin[pl.ds(0, HOMEB)] = (
            part[:, z].astype(F32) + b2p[r].astype(F32) + b2m[r].astype(F32)
        ).astype(BF)

        @pl.loop(0, N_FSDP)
        def _(o):
            snd[r, o] = fin[idx[1 if mixed else 0, o]]

        if mixed:
            @pl.loop(1, N_FSDP)
            def _(i):
                ex_send((h + 5 * i) % N_FSDP).start()

            @pl.when(y // 2 != core)
            def _():
                ex_send(h).start()

            @pl.when(y // 2 == core)
            def _():
                grad[y % 2, rows_of(2 * x + core, r)] = snd[r, h]
        else:
            rcv[r, h] = snd[r, h]

            @pl.loop(1, N_FSDP)
            def _(i):
                plane_send(r, (h + 5 * i) % N_FSDP).start()

    def stage_d(r):
        arrived(rcv.at[r, pl.ds(0, N_FSDP - 1)], pl_r.at[r])
        grad[:, rows_of(d, r)] = rcv[r, pl.ds(2 * d, 2)]

        @pl.loop(1, N_DP)
        def _(i):
            dp_send(r, (d + 3 * i) % N_DP).start()

    def roots_before(t):
        return jnp.where(t < 3, 0, jnp.where(t == 3, 1, jnp.where(t == 4, 3, jnp.where(t == 5, 5, ROOT_STEPS))))

    def either(t, *steps):
        return functools.reduce(jnp.logical_or, [t == step for step in steps])

    stage_a0()

    @pl.loop(1, STEPS)
    def _(t):
        @pl.when(t < R)
        def _():
            stage_a(jnp.where(t == 1, LAST, t - 1))

        @pl.when(either(t, 2, 3))
        def _():
            begin_z(t - 1, False)

        @pl.when(t == 1)
        def _():
            begin_x()

        @pl.when(t == 2)
        def _():
            begin()

        @pl.when(either(t, 2, 3, 4))
        def _():
            stage_b(t - 2, False)

        @pl.when(either(t, 4, 5, 6))
        def _():
            stage_c(t - 4, False)

        @pl.when(t == 4)
        def _():
            end_x()

        @pl.when(t == 5)
        def _():
            stage_b(LAST, True)

        @pl.when(t == 7)
        def _():
            stage_c(LAST, True)

        @pl.when(either(t, 5, 6, 7))
        def _():
            stage_d(t - 5)

        @pl.loop(roots_before(t), roots_before(t + 1))
        def _(step):
            root_step(step)

    arrived(rcv.at[pl.ds(0, LAST), pl.ds(0, 2 * N_DP - 2)], dp_r)

    @pl.when(y // 2 == core)
    def _():
        arrived(snd.at[LAST, pl.ds(0, N_FSDP - 1)], ex_r)

    @pl.when(y // 2 != core)
    def _():
        arrived(snd.at[LAST], ex_r)

    @pl.loop(0, 2)
    def _(j):
        g = grad[j]
        half = dot(keep[0, j], g).astype(BF)
        direction = dot(half, keep[1, j])
        g = g.astype(F32)
        count = float(BS * BS)
        grad_sq = jnp.sum(jnp.sum(g * g, axis=0, keepdims=True), axis=1, keepdims=True)
        dir_sq = jnp.sum(jnp.sum(direction * direction, axis=0, keepdims=True), axis=1, keepdims=True)
        ratio = jnp.sqrt(grad_sq / count) / jnp.sqrt(dir_sq / count + 1e-06)
        upd[j] = (-learn_rate * direction * ratio).astype(BF)
        for p in range(PIECES):
            turn[2 * d + j, p] = upd[j, piece(d, p)]

    @pl.loop(0, PIECES)
    def _(p):
        @pl.loop(1, N_DP)
        def _(i):
            for j in range(2):
                h1_send(j, p, (d + 3 * i) % N_DP).start()

    def forward(i, j, p):
        x = (d + 5 * i) % N_DP
        g = 2 * x + j

        @pl.when(i > 0)
        def _():
            arrived(turn.at[g, p], h1_r.at[g, p])

        @pl.when(g != h)
        def _():
            h2_send(g, p).start()

        @pl.when(g == h)
        def _():
            back[h, p] = turn[h, p]

    @pl.loop(0, PIECES)
    def _(p):
        @pl.loop(0, N_DP)
        def _(i):
            for j in range(2):
                forward(i, j, p)

    @pl.loop(0, 2)
    def _(j):
        g = grad[j]
        st[0, j] = decay_rate * st[0, j] + (1.0 - decay_rate) * dot(g, g, 1, 1)
        st[1, j] = decay_rate * st[1, j] + (1.0 - decay_rate) * dot(g, g, 0, 0)

    arrived(turn.at[pl.ds(0, N_FSDP - 1)], h2_r)

    left(own, 0)
    left(own.at[pl.ds(0, R - 1)], 1)
    left(mix.at[:, pl.ds(0, 3)], 2)
    left(snd.at[pl.ds(0, LAST), pl.ds(0, N_FSDP - 1)], 3)
    left(rcv.at[pl.ds(0, LAST), pl.ds(0, 2 * N_DP - 2)], 4)

    @pl.when(y // 2 == core)
    def _():
        left(snd.at[LAST, pl.ds(0, N_FSDP - 1)], 5)

    @pl.when(y // 2 != core)
    def _():
        left(snd.at[LAST], 5)

    left(upd.at[:, pl.ds(0, BS - ROWS)], 6)
    left(turn.at[pl.ds(0, N_FSDP - 1)], 7)


def finish(owner_in, back, st, keep, updates, out_sl, out_sr, out_rl, out_rr, owner, sem):
    h = lax.axis_index("fsdp")
    table = pltpu.make_async_copy(owner_in, owner, sem.at[8])
    table.start()
    copies = []
    for i in range(2):
        for j in range(2):
            copies.append(pltpu.make_async_copy(st.at[i, j], (out_sl, out_sr)[i].at[j], sem.at[2 * i + j]))
            copies.append(pltpu.make_async_copy(keep.at[i, j], (out_rl, out_rr)[i].at[j], sem.at[4 + 2 * i + j]))
    for copy in copies:
        copy.start()
    table.wait()
    for k in range(HOMEB):
        copies.append(pltpu.make_async_copy(back.at[owner[h * HOMEB + k]], updates.at[k], sem.at[9 + k]))
        copies[-1].start()
    for copy in copies:
        copy.wait()


def local(grads, owner, roster, left_stats, right_stats, left_root, right_root):
    anywhere = pl.BlockSpec(memory_space=pl.ANY)
    dma = pltpu.SemaphoreType.DMA
    shape = jax.ShapeDtypeStruct
    outs = pl.pallas_call(
        kernel,
        out_shape=(
            pltpu.VMEM((N_FSDP, PIECES, PIECE, BS), BF),
            pltpu.VMEM((2, 2, BS, BS), F32),
            pltpu.VMEM((2, 2, BS, BS), BF),
        ),
        in_specs=[anywhere] * 7,
        out_specs=[pl.BlockSpec(memory_space=pltpu.VMEM)] * 3,
        scratch_shapes=[
            pltpu.VMEM((R, HOMEB, NZ, RR, BS), BF),
            pltpu.VMEM((R, HOMEB, NZ, RR, BS), BF),
            pltpu.VMEM((HOMEB, NZ, RR, BS), BF),
            pltpu.VMEM((R, HALF, RR, BS), BF),
            pltpu.VMEM((R, HALF, RR, BS), BF),
            pltpu.VMEM((R, HOMEB, RR, BS), BF),
            pltpu.VMEM((R, HOMEB, RR, BS), BF),
            pltpu.VMEM((HOMEB + 1, RR, BS), BF),
            pltpu.VMEM((R, N_FSDP, RR, BS), BF),
            pltpu.VMEM((R, N_FSDP, RR, BS), BF),
            pltpu.VMEM((2, BS, BS), BF),
            pltpu.VMEM((2, BS, BS), BF),
            pltpu.VMEM((2, BS, BS), BF),
            pltpu.VMEM((2, BS, BS), BF),
            pltpu.VMEM((2, BS, BS), BF),
            pltpu.VMEM((N_FSDP, PIECES, PIECE, BS), BF),
            pltpu.SMEM((2, N_FSDP), jnp.int32),
            pltpu.SMEM((N_FSDP * HOMEB,), jnp.int32),
            pltpu.SMEM((N_FSDP * HOMEB,), jnp.int32),
            dma((R,)),
            dma((6,)),
            dma((8,)),
            dma((NZ,)),
            dma((R,)),
            dma,
            dma((3, R)),
            dma((LAST,)),
            dma,
            dma,
            dma((N_FSDP, PIECES)),
            dma,
        ],
        compiler_params=pltpu.CompilerParams(
            collective_id=0, has_side_effects=True, vmem_limit_bytes=40 * 1024 * 1024
        ),
        cost_estimate=pl.CostEstimate(flops=16 * 10**9, bytes_accessed=24 * 10**6, transcendentals=0),
        name="shampoo",
    )(
        *[
            pltpu.with_memory_space_constraint(array, pltpu.HBM)
            for array in (
                grads.reshape(HOMEB, NZ, 2, R, RR, BS), owner, roster,
                left_stats[0, 0], right_stats[0, 0], left_root[0, 0], right_root[0, 0],
            )
        ],
    )
    result, new_left, new_right, roots_left, roots_right = pl.pallas_call(
        finish,
        out_shape=(
            shape((HOMEB, PIECES, PIECE, BS), BF),
            shape((2, BS, BS), F32),
            shape((2, BS, BS), F32),
            shape((2, BS, BS), BF),
            shape((2, BS, BS), BF),
        ),
        in_specs=[anywhere] * 4,
        out_specs=[anywhere] * 5,
        scratch_shapes=[pltpu.SMEM((N_FSDP * HOMEB,), jnp.int32), dma((9 + HOMEB,))],
        compiler_params=pltpu.CompilerParams(vmem_limit_bytes=2 * 1024 * 1024),
        name="finish",
    )(
        pltpu.with_memory_space_constraint(owner, pltpu.HBM),
        *[pltpu.with_memory_space_constraint(out, pltpu.VMEM) for out in outs],
    )
    result = result.reshape(HOMEB, ROWS, BS)
    return (result, new_left[None, None], new_right[None, None], roots_left[None, None], roots_right[None, None])


def solution(mesh):
    placed = P("dp", "fsdp", None, None, None)
    return jax.shard_map(
        local,
        mesh=mesh,
        in_specs=(P("dp", "fsdp", None, None), P(), P(), placed, placed, placed, placed),
        out_specs=(P("fsdp", "dp", None), placed, placed, placed, placed),
        check_vma=False,
    )
```

```python
import functools

import jax
import jax.numpy as jnp
from jax import lax
from jax.experimental import pallas as pl
from jax.experimental.pallas import tpu as pltpu
from jax.sharding import PartitionSpec as P

BS = 512
HOMEB = 14
HALF = HOMEB // 2
NZ = 4
N_DP = 8
N_FSDP = 16
ROWS = BS // N_DP
R = 4
RR = ROWS // R
LAST = R - 1
ROOT_STEPS = 6
STEPS = 8
PIECES = 4
PIECE = ROWS // PIECES
decay_rate = 0.9
learn_rate = 10.0
BF = jnp.bfloat16
F32 = jnp.float32
MESH = pl.DeviceIdType.MESH


def dot(a, b, ca=1, cb=0):
    return lax.dot_general(a, b, (((ca,), (cb,)), ((), ())), preferred_element_type=F32)


def kernel(
    grads, owner_in, roster_in, left_stats, right_stats, left_root, right_root,
    back, st, keep,
    own, peer, mix, b1p, b1m, b2p, b2m, fin, snd, rcv, grad,
    mat, fac, cur, upd, turn, idx, owner, roster,
    own_sem, in_sem, sent, first_r, core_r, x_r, z_r, pl_r, dp_r, ex_r, h1_r, h2_r,
):
    d = lax.axis_index("dp")
    h = lax.axis_index("fsdp")
    z = d // 2
    core = d % 2
    x = h // 4
    y = h % 4
    up = (z + 1) % NZ
    down = (z + 3) % NZ
    far = (z + 2) % NZ

    def at_dp(x):
        return {"dp": x, "fsdp": h}

    def at_fsdp(x):
        return {"dp": d, "fsdp": x}

    def own_copy(r):
        return pltpu.make_async_copy(grads.at[:, :, core, r], own.at[r], own_sem.at[r])

    def remote(src, dst, s, r, dev):
        return pltpu.make_async_remote_copy(
            src_ref=src, dst_ref=dst, send_sem=s, recv_sem=r, device_id=dev, device_id_type=MESH
        )

    def core_copy(r):
        return remote(grads.at[:, :, 1 - core, r], peer.at[r], sent.at[0], core_r.at[r], at_dp(2 * z + 1 - core))

    def first_copy(i):
        q = (far, up, down, z)[i]
        return remote(
            grads.at[:, q, 1 - core, 0], peer.at[0, :, q], sent.at[0], first_r.at[i], at_dp(2 * z + 1 - core)
        )

    dev_up = at_dp(2 * up + core)
    dev_down = at_dp(2 * down + core)
    lo = pl.ds(0, HALF)
    hi = pl.ds(HALF, HALF)

    def held(r, mixed):
        return mix if mixed else own.at[r]

    def z_copy(kind, r, mixed):
        part = held(r, mixed)
        if kind == 0:
            src, dst, dev = part.at[lo, far], b1p.at[r], dev_up
        elif kind == 1:
            src, dst, dev = part.at[hi, far], b1m.at[r], dev_down
        elif kind == 2:
            src, dst, dev = part.at[hi, up], b2p.at[r, hi], dev_up
        elif kind == 3:
            src, dst, dev = part.at[lo, down], b2m.at[r, lo], dev_down
        elif kind == 4:
            src, dst, dev = part.at[lo, up], b2p.at[r, lo], dev_up
        else:
            src, dst, dev = part.at[hi, down], b2m.at[r, hi], dev_down
        return remote(src, dst, sent.at[1], z_r.at[min(kind, 2), r], dev)

    def x_send(i):
        q = (x + i) % 4
        return remote(own.at[LAST, :, q], mix.at[:, x], sent.at[2], x_r, at_fsdp(4 * q + y))

    def arrived(ref, semaphore):
        remote(ref, ref, sent.at[0], semaphore, dev_up).wait_recv()

    def left(ref, kind):
        remote(ref, ref, sent.at[kind], x_r, dev_up).wait_send()

    def plane_send(r, o):
        return remote(snd.at[r, o], rcv.at[r, h], sent.at[3], pl_r.at[r], at_fsdp(o))

    def rows_of(x, r):
        return pl.ds(pl.multiple_of(x * ROWS + r * RR, RR), RR)

    def dp_send(r, x):
        return remote(rcv.at[r, pl.ds(2 * x, 2)], grad.at[:, rows_of(d, r)], sent.at[4], dp_r, at_dp(x))

    def ex_send(o):
        return remote(
            snd.at[LAST, o], grad.at[y % 2, rows_of(2 * x + core, LAST)], sent.at[5], ex_r,
            {"dp": 2 * z + y // 2, "fsdp": o},
        )

    def chunk(x):
        return pl.ds(pl.multiple_of(x * ROWS, ROWS), ROWS)

    def piece(x, p):
        return pl.ds(pl.multiple_of(x * ROWS + p * PIECE, PIECE), PIECE)

    def h1_send(p, x):
        return remote(upd.at[:, piece(x, p)], turn.at[pl.ds(2 * d, 2), p], sent.at[6], h1_r.at[d, p], at_dp(x))

    def h2_send(g, p):
        return remote(turn.at[g, p], back.at[h, p], sent.at[7], h2_r, at_fsdp(g))

    def stat_in(i):
        return pltpu.make_async_copy((left_stats, right_stats)[i], st.at[i], in_sem.at[i])

    def keep_in(i):
        return pltpu.make_async_copy((left_root, right_root)[i], keep.at[i], in_sem.at[2 + i])

    tables = [
        pltpu.make_async_copy(owner_in, owner, in_sem.at[4]),
        pltpu.make_async_copy(roster_in, roster, in_sem.at[5]),
    ]
    for table in tables:
        table.start()

    @pl.loop(0, R)
    def _(r):
        own_copy(r).start()

    barrier = pltpu.get_barrier_semaphore()

    @pl.loop(0, N_DP)
    def _(i):
        there = {"dp": 2 * z + 1 - core, "fsdp": (i // 2) * 4 + 2 * core + i % 2}
        pl.semaphore_signal(barrier, inc=1, device_id=there, device_id_type=MESH)

    @pl.loop(1, N_FSDP)
    def _(i):
        pl.semaphore_signal(barrier, inc=1, device_id=at_fsdp((h + 5 * i) % N_FSDP), device_id_type=MESH)

    @pl.loop(1, N_DP)
    def _(i):
        pl.semaphore_signal(barrier, inc=1, device_id=at_dp((d + 3 * i) % N_DP), device_id_type=MESH)

    for i in range(2):
        stat_in(i).start()
    for i in range(2):
        keep_in(i).start()
    for table in tables:
        table.wait()

    @pl.loop(0, N_FSDP)
    def _(o):
        for i, home in enumerate((h, 4 * z + y)):
            place = jnp.int32(HOMEB)
            for k in range(HOMEB):
                place = jnp.where(owner[home * HOMEB + k] == o, jnp.int32(k), place)
            idx[i, o] = place

    fin[HOMEB] = jnp.zeros((RR, BS), BF)

    pl.semaphore_wait(barrier, N_DP + N_FSDP - 2 + jnp.where(y // 2 == core, 0, N_FSDP))

    for i in range(NZ):
        first_copy(i).start()
    core_copy(LAST).start()

    def begin():
        for i in range(2):
            stat_in(i).wait()
        for i in range(2):
            keep_in(i).wait()

    ii = lax.broadcasted_iota(jnp.int32, (BS, BS), 0)
    jj = lax.broadcasted_iota(jnp.int32, (BS, BS), 1)

    def factor(m):
        return (jnp.where(ii == jj, 1.25, 0.0) - 0.25 * m).astype(BF)

    def root_step(t):
        slot = t // 3
        sweep = t % 3

        @pl.when(sweep == 0)
        def _():
            for i in range(2):
                a = st[i, slot]
                bound = jnp.max(jnp.sum(jnp.abs(a), axis=0, keepdims=True), axis=1, keepdims=True)
                m = a * (1.0 / bound)
                f = factor(m)
                mat[i] = m.astype(BF)
                fac[i] = f
                first = lax.rsqrt(jnp.sqrt(bound)).astype(BF).astype(F32)
                cur[i] = (first * f.astype(F32)).astype(BF)

        for i in range(2):
            f = fac[i]
            f2 = dot(f, f).astype(BF)
            f4 = dot(f2, f2).astype(BF)
            m = dot(f4, mat[i])
            mat[i] = m.astype(BF)
            f = factor(m)
            fac[i] = f
            cur[i] = dot(cur[i], f).astype(BF)

        @pl.when(sweep == 2)
        def _():
            flag = jnp.int32(0)
            for k in range(HOMEB):
                spot = (2 * d + slot) * HOMEB + k
                flag += jnp.where(owner[spot] == h, roster[spot], 0)
            for i in range(2):
                keep[i, slot] = jnp.where(flag > 0, cur[i], keep[i, slot])

    def stage_a(r):
        own_copy(r).wait()
        core_copy(r).wait_recv()

        @pl.when(r == LAST)
        def _():
            core_copy(2).start()

        @pl.loop(0, HOMEB)
        def _(k):
            own[r, k] = own[r, k] + peer[r, k]

    def stage_a0():
        own_copy(0).wait()
        for i, q in enumerate((far, up, down, z)):
            first_copy(i).wait_recv()
            own[0, :, q] = own[0, :, q] + peer[0, :, q]
            for kind in ((0, 1), (2,), (3,), ())[i]:
                z_copy(kind, 0, False).start()
        core_copy(1).start()

    def begin_z(r, mixed):
        for kind in range(2):
            z_copy(kind, r, mixed).start()

        @pl.when(r < 2)
        def _():
            for kind in range(2, 4):
                z_copy(kind, r, mixed).start()

    def begin_x():
        for i in (2, 1, 3):
            x_send(i).start()
        mix[:, x] = own[LAST, :, x]

    def end_x():
        arrived(mix.at[:, pl.ds(0, 3)], x_r)
        begin_z(LAST, True)
        for kind in range(2, 4):
            z_copy(kind, 2, False).start()
            z_copy(kind, LAST, True).start()

    def stage_b(r, mixed):
        part = held(r, mixed)
        z_copy(0, r, mixed).wait_recv()
        part[lo, up] = part[lo, up] + b1p[r]
        z_copy(4, r, mixed).start()
        z_copy(1, r, mixed).wait_recv()
        part[hi, down] = part[hi, down] + b1m[r]
        z_copy(5, r, mixed).start()

    def stage_c(r, mixed):
        part = held(r, mixed)
        arrived(peer.at[r, lo], z_r.at[2, r])

        fin[pl.ds(0, HOMEB)] = (
            part[:, z].astype(F32) + b2p[r].astype(F32) + b2m[r].astype(F32)
        ).astype(BF)

        @pl.loop(0, N_FSDP)
        def _(o):
            snd[r, o] = fin[idx[1 if mixed else 0, o]]

        if mixed:
            @pl.loop(1, N_FSDP)
            def _(i):
                ex_send((h + 5 * i) % N_FSDP).start()

            @pl.when(y // 2 != core)
            def _():
                ex_send(h).start()

            @pl.when(y // 2 == core)
            def _():
                grad[y % 2, rows_of(2 * x + core, r)] = snd[r, h]
        else:
            rcv[r, h] = snd[r, h]

            @pl.loop(1, N_FSDP)
            def _(i):
                plane_send(r, (h + 5 * i) % N_FSDP).start()

    def stage_d(r):
        arrived(rcv.at[r, pl.ds(0, N_FSDP - 1)], pl_r.at[r])
        grad[:, rows_of(d, r)] = rcv[r, pl.ds(2 * d, 2)]

        @pl.loop(1, N_DP)
        def _(i):
            dp_send(r, (d + 3 * i) % N_DP).start()

    def roots_before(t):
        return jnp.where(t < 3, 0, jnp.where(t == 3, 1, jnp.where(t == 4, 3, jnp.where(t == 5, 5, ROOT_STEPS))))

    def either(t, *steps):
        return functools.reduce(jnp.logical_or, [t == step for step in steps])

    stage_a0()

    @pl.loop(1, STEPS)
    def _(t):
        @pl.when(t < R)
        def _():
            stage_a(jnp.where(t == 1, LAST, t - 1))

        @pl.when(either(t, 2, 3))
        def _():
            begin_z(t - 1, False)

        @pl.when(t == 1)
        def _():
            begin_x()

        @pl.when(t == 2)
        def _():
            begin()

        @pl.when(either(t, 2, 3, 4))
        def _():
            stage_b(t - 2, False)

        @pl.when(either(t, 4, 5, 6))
        def _():
            stage_c(t - 4, False)

        @pl.when(t == 4)
        def _():
            end_x()

        @pl.when(t == 5)
        def _():
            stage_b(LAST, True)

        @pl.when(t == 7)
        def _():
            stage_c(LAST, True)

        @pl.when(either(t, 5, 6, 7))
        def _():
            stage_d(t - 5)

        @pl.loop(roots_before(t), roots_before(t + 1))
        def _(step):
            root_step(step)

    arrived(rcv.at[pl.ds(0, LAST), pl.ds(0, 2 * N_DP - 2)], dp_r)

    @pl.when(y // 2 == core)
    def _():
        arrived(snd.at[LAST, pl.ds(0, N_FSDP - 1)], ex_r)

    @pl.when(y // 2 != core)
    def _():
        arrived(snd.at[LAST], ex_r)

    @pl.loop(0, 2)
    def _(j):
        g = grad[j]
        half = dot(keep[0, j], g).astype(BF)
        direction = dot(half, keep[1, j])
        g = g.astype(F32)
        count = float(BS * BS)
        grad_sq = jnp.sum(jnp.sum(g * g, axis=0, keepdims=True), axis=1, keepdims=True)
        dir_sq = jnp.sum(jnp.sum(direction * direction, axis=0, keepdims=True), axis=1, keepdims=True)
        ratio = jnp.sqrt(grad_sq / count) / jnp.sqrt(dir_sq / count + 1e-06)
        upd[j] = (-learn_rate * direction * ratio).astype(BF)
        for p in range(PIECES):
            turn[2 * d + j, p] = upd[j, piece(d, p)]

    @pl.loop(0, PIECES)
    def _(p):
        @pl.loop(1, N_DP)
        def _(i):
            h1_send(p, (d + 3 * i) % N_DP).start()

    def forward(x, j, p):
        g = 2 * x + j

        @pl.when(g != h)
        def _():
            h2_send(g, p).start()

        @pl.when(g == h)
        def _():
            back[h, p] = turn[h, p]

    @pl.loop(0, PIECES)
    def _(p):
        @pl.loop(0, N_DP)
        def _(i):
            x = (d + 5 * i) % N_DP

            @pl.when(i > 0)
            def _():
                arrived(turn.at[pl.ds(2 * x, 2), p], h1_r.at[x, p])

            for j in range(2):
                forward(x, j, p)

    @pl.loop(0, 2)
    def _(j):
        g = grad[j]
        st[0, j] = decay_rate * st[0, j] + (1.0 - decay_rate) * dot(g, g, 1, 1)
        st[1, j] = decay_rate * st[1, j] + (1.0 - decay_rate) * dot(g, g, 0, 0)

    arrived(turn.at[pl.ds(0, N_FSDP - 1)], h2_r)

    left(own, 0)
    left(own.at[pl.ds(0, R - 1)], 1)
    left(mix.at[:, pl.ds(0, 3)], 2)
    left(snd.at[pl.ds(0, LAST), pl.ds(0, N_FSDP - 1)], 3)
    left(rcv.at[pl.ds(0, LAST), pl.ds(0, 2 * N_DP - 2)], 4)

    @pl.when(y // 2 == core)
    def _():
        left(snd.at[LAST, pl.ds(0, N_FSDP - 1)], 5)

    @pl.when(y // 2 != core)
    def _():
        left(snd.at[LAST], 5)

    left(upd.at[:, pl.ds(0, BS - ROWS)], 6)
    left(turn.at[pl.ds(0, N_FSDP - 1)], 7)


def finish(owner_in, back, st, keep, updates, out_sl, out_sr, out_rl, out_rr, owner, sem):
    h = lax.axis_index("fsdp")
    table = pltpu.make_async_copy(owner_in, owner, sem.at[8])
    table.start()
    copies = []
    for i in range(2):
        for j in range(2):
            copies.append(pltpu.make_async_copy(st.at[i, j], (out_sl, out_sr)[i].at[j], sem.at[2 * i + j]))
            copies.append(pltpu.make_async_copy(keep.at[i, j], (out_rl, out_rr)[i].at[j], sem.at[4 + 2 * i + j]))
    for copy in copies:
        copy.start()
    table.wait()
    for k in range(HOMEB):
        copies.append(pltpu.make_async_copy(back.at[owner[h * HOMEB + k]], updates.at[k], sem.at[9 + k]))
        copies[-1].start()
    for copy in copies:
        copy.wait()


def local(grads, owner, roster, left_stats, right_stats, left_root, right_root):
    anywhere = pl.BlockSpec(memory_space=pl.ANY)
    dma = pltpu.SemaphoreType.DMA
    shape = jax.ShapeDtypeStruct
    outs = pl.pallas_call(
        kernel,
        out_shape=(
            pltpu.VMEM((N_FSDP, PIECES, PIECE, BS), BF),
            pltpu.VMEM((2, 2, BS, BS), F32),
            pltpu.VMEM((2, 2, BS, BS), BF),
        ),
        in_specs=[anywhere] * 7,
        out_specs=[pl.BlockSpec(memory_space=pltpu.VMEM)] * 3,
        scratch_shapes=[
            pltpu.VMEM((R, HOMEB, NZ, RR, BS), BF),
            pltpu.VMEM((R, HOMEB, NZ, RR, BS), BF),
            pltpu.VMEM((HOMEB, NZ, RR, BS), BF),
            pltpu.VMEM((R, HALF, RR, BS), BF),
            pltpu.VMEM((R, HALF, RR, BS), BF),
            pltpu.VMEM((R, HOMEB, RR, BS), BF),
            pltpu.VMEM((R, HOMEB, RR, BS), BF),
            pltpu.VMEM((HOMEB + 1, RR, BS), BF),
            pltpu.VMEM((R, N_FSDP, RR, BS), BF),
            pltpu.VMEM((R, N_FSDP, RR, BS), BF),
            pltpu.VMEM((2, BS, BS), BF),
            pltpu.VMEM((2, BS, BS), BF),
            pltpu.VMEM((2, BS, BS), BF),
            pltpu.VMEM((2, BS, BS), BF),
            pltpu.VMEM((2, BS, BS), BF),
            pltpu.VMEM((N_FSDP, PIECES, PIECE, BS), BF),
            pltpu.SMEM((2, N_FSDP), jnp.int32),
            pltpu.SMEM((N_FSDP * HOMEB,), jnp.int32),
            pltpu.SMEM((N_FSDP * HOMEB,), jnp.int32),
            dma((R,)),
            dma((6,)),
            dma((8,)),
            dma((NZ,)),
            dma((R,)),
            dma,
            dma((3, R)),
            dma((LAST,)),
            dma,
            dma,
            dma((N_DP, PIECES)),
            dma,
        ],
        compiler_params=pltpu.CompilerParams(
            collective_id=0, has_side_effects=True, vmem_limit_bytes=40 * 1024 * 1024
        ),
        cost_estimate=pl.CostEstimate(flops=16 * 10**9, bytes_accessed=24 * 10**6, transcendentals=0),
        name="shampoo",
    )(
        *[
            pltpu.with_memory_space_constraint(array, pltpu.HBM)
            for array in (
                grads.reshape(HOMEB, NZ, 2, R, RR, BS), owner, roster,
                left_stats[0, 0], right_stats[0, 0], left_root[0, 0], right_root[0, 0],
            )
        ],
    )
    result, new_left, new_right, roots_left, roots_right = pl.pallas_call(
        finish,
        out_shape=(
            shape((HOMEB, PIECES, PIECE, BS), BF),
            shape((2, BS, BS), F32),
            shape((2, BS, BS), F32),
            shape((2, BS, BS), BF),
            shape((2, BS, BS), BF),
        ),
        in_specs=[anywhere] * 4,
        out_specs=[anywhere] * 5,
        scratch_shapes=[pltpu.SMEM((N_FSDP * HOMEB,), jnp.int32), dma((9 + HOMEB,))],
        compiler_params=pltpu.CompilerParams(vmem_limit_bytes=2 * 1024 * 1024),
        name="finish",
    )(
        pltpu.with_memory_space_constraint(owner, pltpu.HBM),
        *[pltpu.with_memory_space_constraint(out, pltpu.VMEM) for out in outs],
    )
    result = result.reshape(HOMEB, ROWS, BS)
    return (result, new_left[None, None], new_right[None, None], roots_left[None, None], roots_right[None, None])


def solution(mesh):
    placed = P("dp", "fsdp", None, None, None)
    return jax.shard_map(
        local,
        mesh=mesh,
        in_specs=(P("dp", "fsdp", None, None), P(), P(), placed, placed, placed, placed),
        out_specs=(P("fsdp", "dp", None), placed, placed, placed, placed),
        check_vma=False,
    )
```
